512 devices in a mesh: blk: 16 (over y, x_lo), rep: 32 (over z, x_hi, core).
Axes of the slice: x: 4 (x_hi: 2, x_lo: 2; x = x_hi * 2 + x_lo), y: 8, z: 8, core: 2. Of those that a mesh axis runs over, the one named last changes fastest.
Arguments:
- hamiltonian: float32 [3072, 64, 768], P(('blk', 'rep')), as said below
- pattern: int32 [3072, 12], P(('blk', 'rep')), may hold values from 0 to 1, as said below
Outputs:
- sign_matrix: float32 [3072, 64, 768], P(('blk', 'rep'))
The draws below stay inside these ranges and needn't reach their ends.
Inputs may be any that keep to these rules, and one draw needn't show every extreme that they name: pattern is symmetric: pattern[i, 6 + w] equals pattern[i + w, 6 - w] (block indices modulo 3072); the diagonal position 6 is always 1 and position 0 always 0. hamiltonian is symmetric in the sense of its meaning, and block position 0 is zero.
All inputs are finite; a program needn't handle non-finite values.
Results may differ from the reference program's by a relative error of at most 0.0001.
Values sent between devices are 32-bit elements; how exact they have to be, the bound alone decides.
No kernel may reach another device: no remote copies, remote signals or barrier semaphores. Data moves between devices by JAX's collectives and lax.ppermute only.
A program may use at most 128 MiB of HBM per device.

```python
import math
import jax
import jax.numpy as jnp
from jax import lax

BS = 64
HALF = 6
BAND = 12
ITERS = 2
NB = 3072


def draw_hamiltonian(key, part):
    key = jax.random.fold_in(key, 11)
    first_key, second_key = jax.random.split(key, 2)
    positions = jnp.arange(NB, dtype=jnp.float32) / max(NB - 1, 1)
    upper = jax.random.normal(first_key, (HALF, NB, BS, BS), jnp.float32)
    growth = 1.0 + 2.0 * positions
    orbital_scale = jnp.exp(jax.random.uniform(second_key, (NB, BS), jnp.float32) * 0.5 * math.log(10.0))
    orbital_scale = orbital_scale * jnp.sqrt(jnp.sqrt(growth))[:, None]
    blocks = [jnp.zeros((NB, BS, BS), jnp.float32)]
    for column in range(1, BAND):
        offset = column - HALF
        if offset < 0:
            block = jnp.swapaxes(jnp.roll(upper[-offset], -offset, axis=0), 1, 2)
        elif offset == 0:
            block = (upper[0] + jnp.swapaxes(upper[0], 1, 2)) / math.sqrt(2.0)
        else:
            block = upper[offset]
        partner_scale = jnp.roll(orbital_scale, -offset, axis=0)
        blocks.append(block * orbital_scale[:, :, None] * partner_scale[:, None, :])
    return jnp.concatenate(blocks, axis=2) / math.sqrt(10.0)


def draw_pattern(key, part):
    key = jax.random.fold_in(key, 5)
    upper = (jax.random.randint(key, (NB, HALF - 1), 0, 4) > 0).astype(jnp.int32)
    columns = [jnp.zeros((NB,), jnp.int32)]
    for column in range(1, BAND):
        offset = column - HALF
        if offset < 0:
            columns.append(jnp.roll(upper[:, -offset - 1], -offset, axis=0))
        elif offset == 0:
            columns.append(jnp.ones((NB,), jnp.int32))
        else:
            columns.append(upper[:, offset - 1])
    return jnp.stack(columns, axis=1)


def setup_inputs(seed: int = 0) -> dict:
    seeds = jax.random.split(jax.random.key(seed), 3)
    hamiltonian = draw_hamiltonian(jax.random.fold_in(seeds[2], 71), 0)
    pattern = draw_pattern(jax.random.fold_in(seeds[2], 71), 0)
    return dict(hamiltonian=hamiltonian, pattern=pattern)


def band_product(left_band, right_band, mask_cols):
    band_cols = left_band.shape[2]
    summed = jnp.zeros(left_band.shape, jnp.float32)
    for offset in range(-HALF, HALF):
        low_block = max(-HALF, -HALF - offset)
        high_block = min(HALF - 1, HALF - 1 - offset)
        source = jnp.roll(right_band, -offset, axis=0)[:, :, (low_block + HALF) * BS:(high_block + HALF + 1) * BS]
        factor = left_band[:, :, (offset + HALF) * BS:(offset + HALF + 1) * BS]
        product_term = jnp.einsum('rab,rbc->rac', factor, source, precision=lax.Precision.HIGHEST)
        first_col = (low_block + offset + HALF) * BS
        summed = summed + jnp.pad(product_term, ((0, 0), (0, 0), (first_col, band_cols - first_col - product_term.shape[2])))
    return summed * mask_cols

def reference(hamiltonian, pattern):
    mask_cols = jnp.repeat(pattern.astype(jnp.float32), BS, axis=1)[:, None, :]
    masked = hamiltonian * mask_cols
    frob_norm = jnp.sqrt(jnp.sum(masked * masked))
    scaling = jnp.sqrt(jnp.float32(NB * BS)) / (3.0 * frob_norm)
    current = scaling * masked
    for iteration in range(ITERS):
        square = band_product(current, current, mask_cols)
        cubic = band_product(current, square, mask_cols)
        current = 0.5 * (3.0 * current - cubic)
    return current / scaling
```

```python
import math

import jax
import jax.numpy as jnp
from jax import lax
from jax.experimental import pallas as pl
from jax.experimental.pallas import tpu as pltpu
from jax.sharding import PartitionSpec as P

BS = 64
AXES = ("blk", "rep")
F32 = jnp.float32
BF16 = jnp.bfloat16
VMEM = pl.BlockSpec(memory_space=pltpu.VMEM)
HBM = pl.BlockSpec(memory_space=pltpu.HBM)


def shift(block, distance):
    n = lax.axis_size(AXES)
    return lax.ppermute(block, AXES, [(i, (i + distance) % n) for i in range(n)])


def zeros(rows, blocks):
    return jnp.zeros((rows, blocks * BS), F32)


def lanes(*parts):
    return jnp.concatenate([p for p in parts if p.shape[1]], axis=1)


def split(x):
    high = x.astype(BF16)
    return high, (x - high.astype(F32)).astype(BF16)


def dot(a, b):
    return lax.dot_general(a, b, (((1,), (0,)), ((), ())), preferred_element_type=F32)


def dot3(a_high, a_low, b_high, b_low):
    return dot(a_high, b_high) + (dot(a_high, b_low) + dot(a_low, b_high))


def put(ref_high, ref_low, start, value):
    high, low = split(value)
    ref_high[start : start + value.shape[0], :] = high
    ref_low[start : start + value.shape[0], :] = low


def masked_rows(x, mask):
    pieces = [
        x[BS * i : BS * (i + 1)] * mask[i : i + 1] for i in range(x.shape[0] // BS)
    ]
    return jnp.concatenate(pieces, axis=0)


def prepare_kernel(h_ref, pat_ref, m_ref, mask_ref, right_ref, left_ref, right2_ref, left2_ref, ssq_ref):
    pat = pat_ref[...].astype(F32)
    owner = lax.broadcasted_iota(jnp.int32, (12, 12 * BS), 1) // BS
    spread = (owner == lax.broadcasted_iota(jnp.int32, (12, 12 * BS), 0)).astype(F32)
    mask = dot(pat, spread)
    mask = jnp.concatenate([mask, jnp.zeros((2, 12 * BS), F32)], axis=0)
    mask_ref[...] = mask
    total = jnp.zeros((8, 128), F32)
    rows = []
    for i in range(6):
        at = slice(BS * i, BS * (i + 1))
        row = h_ref[at, :] * mask[i : i + 1, :]
        m_ref[at, :] = row
        right_ref[at, :] = row[:, 64:448]
        left_ref[at, :] = row[:, 384:768]
        square = row * row
        for a in range(8):
            for b in range(6):
                total = total + square[8 * a : 8 * a + 8, 128 * b : 128 * b + 128]
        rows.append(row)
    upper = lanes(mask[:, 448:768], zeros(8, 1))
    for ref in (right_ref, left_ref):
        ref[384:392, :] = mask[:, 64:448]
        ref[392:400, :] = upper
    right2_ref[...] = lanes(rows[5][:, 192:448], rows[4][:, 256:448], rows[2][:, 384:448], rows[3][:, 320:448])
    left2_ref[...] = lanes(rows[0][:, 384:640], rows[1][:, 384:576], rows[3][:, 384:448], rows[2][:, 384:512])
    ssq_ref[...] = jnp.zeros(ssq_ref.shape, F32) + jnp.sum(total)


def spread_sum_kernel(in_ref, out_ref):
    out_ref[...] = jnp.zeros(out_ref.shape, F32) + jnp.sum(in_ref[...]) / 128.0


def own_window(x):
    n = x.shape[0] // 6 if x.shape[0] > 8 else 1
    out = []
    for i in range(6):
        row = x[n * i : n * (i + 1)]
        if i == 0:
            out.append(lanes(row[:, BS:], zeros(n, 5)))
        else:
            out.append(lanes(zeros(n, i - 1), row, zeros(n, 5 - i)))
    return jnp.concatenate(out, axis=0)


def mirror(a, lower):
    br = lax.broadcasted_iota(jnp.int32, a.shape, 0) // BS
    bc = lax.broadcasted_iota(jnp.int32, a.shape, 1) // BS
    keep = br >= bc if lower else br <= bc
    return jnp.where(keep, a, a.T)


def first_kernel(
    m_ref, mask_ref, fl_ref, fr_ref, fl2_ref, fr2_ref,
    mo_ref, ml_ref, mr_ref, to_ref, tl_ref, tr_ref, ko_ref, kl_ref, kr_ref, g_ref,
    lh, ll, oh, ol, rh, rl,
):
    top = jnp.maximum(jnp.max(jnp.abs(m_ref[...])), jnp.max(jnp.abs(fl_ref[0:384, :])))
    top = jnp.maximum(top, jnp.max(jnp.abs(fr_ref[0:384, :])))
    top = jnp.maximum(top, jnp.max(jnp.abs(fl2_ref[...])))
    top = jnp.maximum(top, jnp.max(jnp.abs(fr2_ref[...])))
    top = jnp.maximum(top, 1e-30)
    g = 1.0 / top
    g_ref[...] = jnp.zeros(g_ref.shape, F32) + top

    fl = fl_ref[0:384, :] * g
    fr = fr_ref[0:384, :] * g
    fl2 = fl2_ref[...] * g
    fr2 = fr2_ref[...] * g
    a = [
        lanes(fl2[:, 448:512], zeros(BS, 9)),
        lanes(fl2[:, 512:640], zeros(BS, 8)),
        lanes(fl2[:, 256:448], zeros(BS, 7)),
        lanes(fl2[:, 0:256], zeros(BS, 6)),
        lanes(fl[0:64, 64:384], zeros(BS, 5)),
    ]
    for i in range(1, 6):
        a.append(lanes(zeros(BS, i - 1), fl[64 * i : 64 * i + 64], zeros(BS, 5 - i)))
    full_l = mirror(jnp.concatenate(a, axis=0), True)
    a = []
    for i in range(5):
        a.append(lanes(zeros(BS, i), fr[64 * i : 64 * i + 64], zeros(BS, 4 - i)))
    a.append(lanes(zeros(BS, 5), fr[320:384, 0:320]))
    a.append(lanes(zeros(BS, 6), fr2[:, 0:256]))
    a.append(lanes(zeros(BS, 7), fr2[:, 256:448]))
    a.append(lanes(zeros(BS, 8), fr2[:, 512:640]))
    a.append(lanes(zeros(BS, 9), fr2[:, 448:512]))
    full_r = mirror(jnp.concatenate(a, axis=0), False)
    own = own_window(m_ref[...] * g)
    cross_l = own[:, 0:384].T[0:320]
    cross_r = own[:, 640:1024].T[64:384]
    halo_l = lanes(zeros(320, 1), full_l[320:640], cross_l[:, 0:320])
    halo_r = lanes(cross_r[:, 64:384], full_r[0:320], zeros(320, 1))
    halo_lo = lanes(full_l[320:640, 320:640], cross_l, zeros(320, 5))
    halo_ro = lanes(zeros(320, 5), cross_r, full_r[0:320, 0:320])
    mo_ref[...] = own
    ml_ref[...] = halo_lo[:, 0:640]
    mr_ref[...] = halo_ro[:, 384:1024]

    put(lh, ll, 0, zeros(64, 16))
    put(lh, ll, 64, lanes(zeros(320, 1), full_l[0:320], zeros(320, 5)))
    put(lh, ll, 384, halo_l)
    put(lh, ll, 704, lanes(zeros(320, 6), own[0:320, 0:640]))
    put(oh, ol, 0, halo_lo)
    put(oh, ol, 320, own)
    put(oh, ol, 704, halo_ro)
    put(rh, rl, 0, lanes(own[64:384, 384:1024], zeros(320, 6)))
    put(rh, rl, 320, halo_r)
    put(rh, rl, 640, lanes(zeros(320, 5), full_r[320:640], zeros(320, 1)))
    put(rh, rl, 960, zeros(64, 16))

    mask_o = own_window(mask_ref[...])
    ko_ref[...] = jnp.concatenate([mask_o, jnp.zeros((2, 1024), F32)], axis=0)
    mask_l, mask_r = [], []
    for i in range(5):
        band = lanes(fl_ref[385 + i : 386 + i, :], fl_ref[393 + i : 394 + i, 0:320])
        mask_l.append(lanes(zeros(1, 1 + i), band, zeros(1, 4 - i)))
        band = lanes(fr_ref[384 + i : 385 + i, :], fr_ref[392 + i : 393 + i, 0:320])
        mask_r.append(lanes(zeros(1, i), band, zeros(1, 5 - i)))
    mask_l = jnp.concatenate(mask_l, axis=0)
    mask_r = jnp.concatenate(mask_r, axis=0)
    pad = jnp.zeros((3, 640), F32)
    kl_ref[...] = jnp.concatenate([mask_l[:, 384:1024], pad], axis=0)
    kr_ref[...] = jnp.concatenate([mask_r[:, 0:640], pad], axis=0)

    s_l = masked_rows(dot3(lh[384:704, :], ll[384:704, :], lh[...], ll[...]), mask_l)
    s_o = masked_rows(dot3(oh[320:704, :], ol[320:704, :], oh[...], ol[...]), mask_o)
    s_r = masked_rows(dot3(rh[320:640, :], rl[320:640, :], rh[...], rl[...]), mask_r)

    ah, al = lh[384:704, :], ll[384:704, :]
    s_left = jnp.concatenate(
        [zeros(64, 10), lanes(s_l[:, 0:384].T[64:384], zeros(320, 5)), s_l[:, 384:1024], s_o[0:320, 0:640]], axis=0
    )
    tl_ref[...] = masked_rows(dot3(ah, al, *split(s_left)), mask_l[:, 384:1024])
    ah, al = rh[320:640, :], rl[320:640, :]
    s_right = jnp.concatenate(
        [s_o[64:384, 384:1024], s_r[:, 0:640], lanes(zeros(320, 5), s_r[:, 640:1024].T[0:320]), zeros(64, 10)], axis=0
    )
    tr_ref[...] = masked_rows(dot3(ah, al, *split(s_right)), mask_r[:, 0:640])
    ah, al = oh[320:704, :], ol[320:704, :]
    s_mid = jnp.concatenate(
        [lanes(s_l[:, 384:1024], zeros(320, 6)), s_o, lanes(zeros(320, 6), s_r[:, 0:640])], axis=0
    )
    to_ref[...] = masked_rows(dot3(ah, al, *split(s_mid)), mask_o)


def second_kernel(
    norms_ref, g_ref, mo_ref, ml_ref, mr_ref, to_ref, tl_ref, tr_ref, ko_ref,
    x_ref, xh, xl, s2_ref, right_ref, left_ref, inv_ref, *, size
):
    frob = jnp.sqrt(jnp.sum(norms_ref[...], keepdims=True)[0] / 128.0)
    inverse = 3.0 * frob / size
    inv_ref[...] = jnp.zeros(inv_ref.shape, F32) + inverse
    r = g_ref[0:1, 0:1] / inverse
    c1 = 1.5 * r
    c3 = 0.5 * r * r * r
    x_o = c1 * mo_ref[...] - c3 * to_ref[...]
    x_ref[...] = x_o
    put(xh, xl, 0, lanes(c1 * ml_ref[...] - c3 * tl_ref[...], zeros(320, 6)))
    put(xh, xl, 320, x_o)
    put(xh, xl, 704, lanes(zeros(320, 6), c1 * mr_ref[...] - c3 * tr_ref[...]))
    s2 = dot3(xh[320:704, :], xl[320:704, :], xh[:, 256:768], xl[:, 256:768])
    s2 = masked_rows(s2, ko_ref[0:6, 256:768])
    s2_ref[...] = s2
    for ref, block in ((right_ref, s2[64:384, 128:448]), (left_ref, s2[0:320, 64:384])):
        ref[0:320, :] = block[:, 0:128]
        ref[320:640, :] = block[:, 128:256]
        ref[640:800, :] = lanes(block[0:160, 256:320], block[160:320, 256:320])


def third_kernel(xh, xl, s2_ref, ko_ref, kl_ref, kr_ref, out_ref):
    ah, al = xh[320:704, :], xl[320:704, :]
    s2_a = masked_rows(dot3(ah, al, xh[:, 0:256], xl[:, 0:256]), ko_ref[0:6, 0:256])
    s2_b = masked_rows(dot3(ah, al, xh[:, 768:1024], xl[:, 768:1024]), ko_ref[0:6, 768:1024])
    s2_l = dot3(xh[0:320, 0:640], xl[0:320, 0:640], xh[0:640, 256:640], xl[0:640, 256:640])
    s2_l = masked_rows(s2_l, kl_ref[0:5, 256:640])[:, 64:384]
    s2_r = dot3(xh[704:1024, 384:1024], xl[704:1024, 384:1024], xh[384:1024, 384:768], xl[384:1024, 384:768])
    s2_r = masked_rows(s2_r, kr_ref[0:5, 0:384])[:, 0:320]
    s2 = jnp.concatenate(
        [
            lanes(zeros(320, 5), s2_l, zeros(320, 6)),
            lanes(s2_a, s2_ref[...], s2_b),
            lanes(zeros(320, 6), s2_r, zeros(320, 5)),
        ],
        axis=0,
    )
    out_ref[...] = dot3(ah, al, *split(s2))


def unpack(ref):
    tail = ref[640:800, :]
    return lanes(ref[0:320, :], ref[320:640, :], jnp.concatenate([tail[:, 0:64], tail[:, 64:128]], axis=0))


def last_kernel(part_ref, x_ref, xh, xl, ko_ref, inv_ref, fl_ref, fr_ref, out_ref):
    corner_l = jnp.concatenate([lanes(unpack(fl_ref), zeros(320, 1)), zeros(64, 6)], axis=0)
    corner_r = jnp.concatenate([zeros(64, 6), lanes(zeros(320, 1), unpack(fr_ref))], axis=0)
    add_l = dot3(xh[320:704, 0:384], xl[320:704, 0:384], *split(corner_l))
    add_r = dot3(xh[320:704, 640:1024], xl[320:704, 640:1024], *split(corner_r))
    cubic = lanes(part_ref[:, 0:384] + add_l, part_ref[:, 384:640], part_ref[:, 640:1024] + add_r)
    inverse = inv_ref[0:1, 0:1]
    for i in range(6):
        at = slice(BS * i, BS * (i + 1))
        row = (1.5 * x_ref[at, :] - 0.5 * (cubic[at] * ko_ref[i : i + 1, :])) * inverse
        if i == 0:
            out_ref[at, :] = lanes(zeros(BS, 1), row[:, 0:704])
        else:
            out_ref[at, :] = row[:, 64 * (i - 1) : 64 * (i - 1) + 768]


def call(kernel, outs, args, flops, name, scratch=(), spaces=None):
    return pl.pallas_call(
        kernel,
        out_shape=[jax.ShapeDtypeStruct(s, t) for s, t in outs],
        in_specs=[VMEM] * len(args),
        out_specs=spaces or [VMEM] * len(outs),
        scratch_shapes=list(scratch),
        compiler_params=pltpu.CompilerParams(vmem_limit_bytes=48 << 20),
        cost_estimate=pl.CostEstimate(flops=flops, bytes_accessed=1 << 20, transcendentals=0),
        name=name,
    )(*args)


def local(hamiltonian, pattern):
    n_blk, n_rep = lax.axis_size("blk"), lax.axis_size("rep")
    size = math.sqrt(n_blk * n_rep * 6 * BS)
    band = hamiltonian.reshape(6 * BS, 12 * BS)
    m, mask, to_right, to_left, to_right2, to_left2, ssq = call(
        prepare_kernel,
        [((384, 768), F32), ((8, 768), F32), ((400, 384), F32), ((400, 384), F32),
         ((64, 640), F32), ((64, 640), F32), ((n_rep, 1, 128), F32)],
        (band, pattern), 10**7, "prepare",
    )
    from_left = shift(to_right, 1)
    from_right = shift(to_left, -1)
    from_left2 = shift(to_right2, 2)
    from_right2 = shift(to_left2, -2)
    ssq = lax.all_to_all(ssq, "rep", 0, 0)
    (ssq,) = call(spread_sum_kernel, [((n_blk, 1, 128), F32)], (ssq,), 10**5, "row_sum")
    ssq = lax.all_to_all(ssq, "blk", 0, 0)
    wide = pltpu.VMEM((1024, 1024), BF16)
    big, halo = ((384, 1024), F32), ((320, 640), F32)
    mo, ml, mr, to, tl, tr, ko, kl, kr, g = call(
        first_kernel,
        [big, halo, halo, big, halo, halo, ((8, 1024), F32), ((8, 640), F32), ((8, 640), F32), ((8, 128), F32)],
        (m, mask, from_left, from_right, from_left2, from_right2), 10**10, "first_iteration",
        scratch=[wide] * 6,
    )
    x, xh, xl, s2, to_right, to_left, inverse = call(
        lambda *refs: second_kernel(*refs, size=size),
        [big, ((1024, 1024), BF16), ((1024, 1024), BF16), ((384, 512), F32),
         ((800, 128), F32), ((800, 128), F32), ((8, 128), F32)],
        (ssq, g, mo, ml, mr, to, tl, tr, ko), 10**9, "second_square",
    )
    from_left = shift(to_right, 1)
    from_right = shift(to_left, -1)
    (part,) = call(third_kernel, [big], (xh, xl, s2, ko, kl, kr), 10**10, "second_cubic")
    (out,) = call(
        last_kernel, [((384, 768), F32)], (part, x, xh, xl, ko, inverse, from_left, from_right), 10**9, "result"
    )
    return out.reshape(6, BS, 12 * BS)


def solution(mesh):
    placed = (P(AXES, None, None), P(AXES, None))
    return jax.shard_map(
        local, mesh=mesh, in_specs=placed, out_specs=P(AXES, None, None), check_vma=False
    )
```

```python
import math

import jax
import jax.numpy as jnp
from jax import lax
from jax.experimental import pallas as pl
from jax.experimental.pallas import tpu as pltpu
from jax.sharding import PartitionSpec as P

BS = 64
AXES = ("blk", "rep")
F32 = jnp.float32
BF16 = jnp.bfloat16
VMEM = pl.BlockSpec(memory_space=pltpu.VMEM)
HBM = pl.BlockSpec(memory_space=pltpu.HBM)


def across(block):
    n = lax.axis_size(AXES)
    return lax.ppermute(block, AXES, [(i, (i + 1 if i % 2 else i - 1) % n) for i in range(n)])


def inside(block):
    n = lax.axis_size(AXES)
    return lax.ppermute(block, AXES, [(i, i ^ 1) for i in range(n)])


def odd():
    return lax.rem(lax.axis_index("rep"), 2) == 1


def zeros(rows, blocks):
    return jnp.zeros((rows, blocks * BS), F32)


def lanes(*parts):
    return jnp.concatenate([p for p in parts if p.shape[1]], axis=1)


def stack(*parts):
    return jnp.concatenate(parts, axis=0)


def split(x):
    high = x.astype(BF16)
    return high, (x - high.astype(F32)).astype(BF16)


def dot(a, b):
    return lax.dot_general(a, b, (((1,), (0,)), ((), ())), preferred_element_type=F32)


def dot3(a_high, a_low, b_high, b_low):
    return dot(a_high, b_high) + (dot(a_high, b_low) + dot(a_low, b_high))


def store(pair, start, value):
    for ref, part in zip(pair, split(value)):
        ref[start : start + value.shape[0], :] = part


def masked_rows(x, mask):
    return stack(*[x[BS * i : BS * (i + 1)] * mask[i : i + 1] for i in range(x.shape[0] // BS)])


def own_product(left, right):
    out = []
    for p in range(3):
        rows, reach = slice(128 * p, 128 * p + 128), slice(128 * p, 128 * p + 768)
        part = dot3(left[0][rows, reach], left[1][rows, reach], right[0][reach, reach], right[1][reach, reach])
        out.append(lanes(zeros(128, 2 * p), part, zeros(128, 4 - 2 * p)))
    return stack(*out)


def own_window(x):
    n = x.shape[0] // 6 if x.shape[0] > 8 else 1
    out = [lanes(x[0:n, BS:], zeros(n, 5))]
    for i in range(1, 6):
        out.append(lanes(zeros(n, i - 1), x[n * i : n * (i + 1)], zeros(n, 5 - i)))
    return stack(*out)


def mirror(a, lower):
    br = lax.broadcasted_iota(jnp.int32, a.shape, 0) // BS
    bc = lax.broadcasted_iota(jnp.int32, a.shape, 1) // BS
    keep = br >= bc if lower else br <= bc
    return jnp.where(keep, a, a.T)


def prepare_kernel(h_hbm, pat_hbm, m_ref, mask_ref, b_ref, a_ref, ssq_hbm, h_ref, pat_ref, ssq_ref, sem):
    fetch_pat = pltpu.make_async_copy(pat_hbm, pat_ref, sem.at[0])
    fetch_h = pltpu.make_async_copy(h_hbm, h_ref, sem.at[1])
    fetch_h.start()
    fetch_pat.start()
    fetch_pat.wait()
    pat = pat_ref[...].astype(F32)
    owner = lax.broadcasted_iota(jnp.int32, (12, 12 * BS), 1) // BS
    spread = (owner == lax.broadcasted_iota(jnp.int32, (12, 12 * BS), 0)).astype(F32)
    mask = stack(dot(pat, spread), jnp.zeros((2, 12 * BS), F32))
    mask_ref[...] = mask
    side = odd()
    for start, part in ((320, mask[:, 64:448]), (328, lanes(mask[:, 448:768], zeros(8, 1)))):
        b_ref[start : start + 8, :] = part
        a_ref[start : start + 8, :] = part
    fetch_h.wait()
    total = jnp.zeros((8, 128), F32)
    rows = []
    for i in range(6):
        at = slice(BS * i, BS * (i + 1))
        row = h_ref[at, :] * mask[i : i + 1, :]
        m_ref[at, :] = row
        square = row * row
        for a in range(8):
            for b in range(6):
                total = total + square[8 * a : 8 * a + 8, 128 * b : 128 * b + 128]
        rows.append(row)
    ssq_ref[...] = jnp.zeros(ssq_ref.shape, F32) + jnp.sum(total)
    send_ssq = pltpu.make_async_copy(ssq_ref, ssq_hbm, sem.at[0])
    send_ssq.start()
    for i in range(5):
        at = slice(BS * i, BS * (i + 1))
        to_right, to_left = rows[i + 1][:, 64:448], rows[i][:, 384:768]
        b_ref[at, :] = jnp.where(side, to_right, to_left)
        a_ref[at, :] = jnp.where(side, to_left, to_right)
    send_ssq.wait()


def fetch(sem, *pairs):
    copies = [pltpu.make_async_copy(source, target, sem.at[i]) for i, (source, target) in enumerate(pairs)]
    for copy in copies:
        copy.start()
    return copies


def halos(across_ref, inside_ref):
    side = odd()
    fb, fa = across_ref[...], inside_ref[...]
    return jnp.where(side, fa, fb), jnp.where(side, fb, fa)


def surroundings(own, fl, fr, g):
    fl, fr = fl[0:320] * g, fr[0:320] * g
    low = stack(*[lanes(zeros(BS, i), fl[BS * i : BS * (i + 1)], zeros(BS, 4 - i)) for i in range(5)])
    high = stack(*[lanes(zeros(BS, i), fr[BS * i : BS * (i + 1)], zeros(BS, 4 - i)) for i in range(5)])
    cross_l = own[:, 0:384].T[0:320]
    cross_r = own[:, 640:1024].T[64:384]
    hl = lanes(zeros(320, 1), low[:, 0:320], mirror(low[:, 320:640], True), cross_l[:, 0:320])
    hr = lanes(cross_r[:, 64:384], mirror(high[:, 0:320], False), high[:, 320:640], zeros(320, 1))
    return hl, hr


def masks(mask_own, fl, fr):
    mask_l, mask_r = [], []
    for i in range(5):
        band = lanes(fl[321 + i : 322 + i], fl[329 + i : 330 + i, 0:320])
        mask_l.append(lanes(zeros(1, 1 + i), band, zeros(1, 4 - i))[:, 384:1024])
        band = lanes(fr[320 + i : 321 + i], fr[328 + i : 329 + i, 0:320])
        mask_r.append(lanes(zeros(1, i), band, zeros(1, 5 - i))[:, 0:640])
    return mask_own if mask_own is None else own_window(mask_own), stack(*mask_l), stack(*mask_r)


def square_kernel(m_ref, mask_ref, b_hbm, a_hbm, s_ref, top_ref, oh, ol, wh, wl, b_ref, a_ref, sem):
    copies = fetch(sem, (b_hbm, b_ref), (a_hbm, a_ref))
    m = m_ref[...]
    own = own_window(m)
    for copy in copies:
        copy.wait()
    fl, fr = halos(b_ref, a_ref)
    top = jnp.maximum(jnp.max(jnp.abs(fl[0:320])), jnp.max(jnp.abs(fr[0:320])))
    top = jnp.maximum(jnp.maximum(top, jnp.max(jnp.abs(m))), 1e-11)
    top_ref[...] = jnp.zeros(top_ref.shape, F32) + top
    own = own * (1.0 / top)
    hl, hr = surroundings(own, fl, fr, 1.0 / top)
    store((oh, ol), 0, own)
    store((wh, wl), 0, lanes(hl[:, 384:1024], zeros(320, 6)))
    store((wh, wl), 320, own)
    store((wh, wl), 704, lanes(zeros(320, 6), hr[:, 0:640]))
    s_ref[...] = masked_rows(own_product((oh, ol), (wh, wl)), own_window(mask_ref[...]))


def send_kernel(ssq_ref, s_ref, top_ref, b_ref, a_ref, new_top_ref, out_hbm, out_ref, sem):
    out_ref[...] = jnp.zeros(out_ref.shape, F32) + jnp.sum(ssq_ref[...]) / 128.0
    copy = pltpu.make_async_copy(out_ref, out_hbm, sem.at[0])
    copy.start()
    side = odd()
    new_top_ref[...] = top_ref[...]
    scale = zeros(BS, 3) + top_ref[0:1, 0:1]
    row = [s_ref[BS * i : BS * (i + 1), :] for i in range(6)]
    to_right = stack(
        lanes(row[1][:, 64:384], row[5][:, 320:384]),
        lanes(row[2][:, 128:384], row[4][:, 256:384]),
        lanes(row[3][:, 192:384], scale),
    )
    to_left = stack(
        lanes(row[4][:, 640:960], row[0][:, 640:704]),
        lanes(row[3][:, 640:896], row[1][:, 640:768]),
        lanes(row[2][:, 640:832], scale),
    )
    b_ref[...] = jnp.where(side, to_right, to_left)
    a_ref[...] = jnp.where(side, to_left, to_right)
    copy.wait()


def halo_square_kernel(top_ref, m_ref, b_hbm, a_hbm, sl_hbm, sr_hbm, b_ref, a_ref, sl_ref, sr_ref, sem):
    copies = fetch(sem, (b_hbm, b_ref), (a_hbm, a_ref))
    g = 1.0 / top_ref[0:1, 0:1]
    own = own_window(m_ref[...]) * g
    for copy in copies:
        copy.wait()
    fl, fr = halos(b_ref, a_ref)
    _, mask_l, mask_r = masks(None, fl, fr)
    hl, hr = surroundings(own, fl, fr, g)
    right = stack(zeros(64, 6), lanes(hl[:, 0:384].T[64:384], zeros(320, 1)), hl[:, 384:768], own[0:320, 0:384])
    s_l = dot3(*split(hl), *split(right))
    sl_ref[...] = masked_rows(s_l[:, 0:320], mask_l[:, 0:320])
    keep_l = pltpu.make_async_copy(sl_ref, sl_hbm, sem.at[0])
    keep_l.start()
    right = stack(own[64:384, 640:1024], hr[:, 256:640], lanes(zeros(320, 1), hr[:, 640:1024].T[0:320]), zeros(64, 6))
    s_r = dot3(*split(hr), *split(right))
    sr_ref[...] = masked_rows(s_r[:, 64:384], mask_r[:, 320:640])
    keep_r = pltpu.make_async_copy(sr_ref, sr_hbm, sem.at[1])
    keep_r.start()
    keep_l.wait()
    keep_r.wait()


def second_kernel(
    norms_ref, top_ref, m_ref, mask_ref, s_ref, b1_hbm, a1_hbm, sl_hbm, sr_hbm, b2_hbm, a2_hbm,
    x_ref, xh, xl, s2_ref, b_ref, a_ref, inv_ref, ko_ref, kl_ref, kr_ref,
    oh, ol, lh, ll, rh, rl, wh, wl, b1_ref, a1_ref, sl_ref, sr_ref, b2_ref, a2_ref, sem, *, size
):
    copies = fetch(
        sem, (b1_hbm, b1_ref), (a1_hbm, a1_ref), (sl_hbm, sl_ref), (sr_hbm, sr_ref), (b2_hbm, b2_ref), (a2_hbm, a2_ref)
    )
    top = top_ref[0:1, 0:1]
    own = own_window(m_ref[...]) * (1.0 / top)
    store((oh, ol), 0, own)
    s = s_ref[...]
    store((wh, wl), 320, s)
    for copy in copies:
        copy.wait()
    fl, fr = halos(b1_ref, a1_ref)
    mask_o, mask_l, mask_r = masks(mask_ref[...], fl, fr)
    ko_ref[...] = stack(mask_o, jnp.zeros((2, 1024), F32))
    kl_ref[...] = stack(mask_l, jnp.zeros((3, 640), F32))
    kr_ref[...] = stack(mask_r, jnp.zeros((3, 640), F32))
    hl, hr = surroundings(own, fl, fr, 1.0 / top)

    store((wh, wl), 0, lanes(sl_ref[...], s[:, 0:384].T[0:320, 0:320], zeros(320, 6)))
    store((wh, wl), 704, lanes(zeros(320, 6), s[:, 640:1024].T[64:384, 64:384], sr_ref[...]))
    t_o = masked_rows(own_product((oh, ol), (wh, wl)), mask_o)
    fl, fr = halos(b2_ref, a2_ref)
    far_l = stack(
        fl[0:64, 0:320],
        lanes(zeros(BS, 1), fl[64:128, 0:256]),
        lanes(zeros(BS, 2), fl[128:192, 0:192]),
        lanes(zeros(BS, 3), fl[64:128, 256:384]),
        lanes(zeros(BS, 4), fl[0:64, 320:384]),
    )
    far_r = stack(
        lanes(fr[0:64, 320:384], zeros(BS, 4)),
        lanes(fr[64:128, 256:384], zeros(BS, 3)),
        lanes(fr[128:192, 0:192], zeros(BS, 2)),
        lanes(fr[64:128, 0:256], zeros(BS, 1)),
        fr[0:64, 0:320],
    )
    ratio_l, ratio_r = fl[128:129, 192:193] / top, fr[128:129, 192:193] / top
    store((lh, ll), 0, zeros(64, 10))
    store((lh, ll), 64, lanes((far_l * ratio_l * ratio_l).T, zeros(320, 5)))
    lh[384:1024, :], ll[384:1024, :] = wh[0:640, 0:640], wl[0:640, 0:640]
    t_l = masked_rows(dot3(*split(hl), lh[...], ll[...]), mask_l)
    rh[0:640, :], rl[0:640, :] = wh[384:1024, 384:1024], wl[384:1024, 384:1024]
    store((rh, rl), 640, lanes(zeros(320, 5), (far_r * ratio_r * ratio_r).T))
    store((rh, rl), 960, zeros(64, 10))
    t_r = masked_rows(dot3(*split(hr), rh[...], rl[...]), mask_r)

    frob = jnp.sqrt(jnp.sum(norms_ref[...], keepdims=True)[0] / 128.0)
    inverse = 3.0 * frob / size
    inv_ref[...] = jnp.zeros(inv_ref.shape, F32) + inverse
    r = top / inverse
    c1 = 1.5 * r
    c3 = 0.5 * r * r * r
    x = c1 * own - c3 * t_o
    x_ref[...] = x
    store((xh, xl), 0, lanes(c1 * hl[:, 384:1024] - c3 * t_l, zeros(320, 6)))
    store((xh, xl), 320, x)
    store((xh, xl), 704, lanes(zeros(320, 6), c1 * hr[:, 0:640] - c3 * t_r))
    s2 = dot3(xh[320:704, :], xl[320:704, :], xh[:, 256:768], xl[:, 256:768])
    s2 = masked_rows(s2, mask_o[:, 256:768])
    s2_ref[...] = s2

    def pack(block):
        tail = lanes(block[0:160, 256:320], block[160:320, 256:320])
        return stack(block[:, 0:128], block[:, 128:256], tail)

    side = odd()
    to_right, to_left = pack(s2[64:384, 128:448]), pack(s2[0:320, 64:384])
    b_ref[...] = jnp.where(side, to_right, to_left)
    a_ref[...] = jnp.where(side, to_left, to_right)


def third_kernel(x_ref, xh, xl, s2_ref, ko_ref, kl_ref, kr_ref, inv_ref, out_ref, wh, wl):
    ah, al = xh[320:704, :], xl[320:704, :]
    s2_a = masked_rows(dot3(ah, al, xh[:, 0:256], xl[:, 0:256]), ko_ref[0:6, 0:256])
    s2_b = masked_rows(dot3(ah, al, xh[:, 768:1024], xl[:, 768:1024]), ko_ref[0:6, 768:1024])
    s2_l = dot3(xh[0:320, 0:640], xl[0:320, 0:640], xh[0:640, 256:640], xl[0:640, 256:640])
    s2_l = masked_rows(s2_l, kl_ref[0:5, 256:640])[:, 64:384]
    s2_r = dot3(xh[704:1024, 384:1024], xl[704:1024, 384:1024], xh[384:1024, 384:768], xl[384:1024, 384:768])
    s2_r = masked_rows(s2_r, kr_ref[0:5, 0:384])[:, 0:320]
    store((wh, wl), 0, lanes(zeros(320, 5), s2_l, zeros(320, 6)))
    store((wh, wl), 320, lanes(s2_a, s2_ref[...], s2_b))
    store((wh, wl), 704, lanes(zeros(320, 6), s2_r, zeros(320, 5)))
    left = (xh.at[320:704, :], xl.at[320:704, :])
    cubic = own_product(left, (wh, wl))
    inverse = inv_ref[0:1, 0:1]
    for i in range(6):
        at = slice(BS * i, BS * (i + 1))
        row = (1.5 * x_ref[at, :] - 0.5 * (cubic[at] * ko_ref[i : i + 1, :])) * inverse
        if i == 0:
            out_ref[at, :] = lanes(zeros(BS, 1), row[:, 0:704])
        else:
            out_ref[at, :] = row[:, 64 * (i - 1) : 64 * (i - 1) + 768]


def last_kernel(part_ref, xh, xl, ko_ref, inv_ref, fb_ref, fa_ref, out_hbm, out_ref, sem):
    side = odd()
    fb, fa = fb_ref[...], fa_ref[...]
    corner_l, corner_r = [
        lanes(f[0:320], f[320:640], stack(f[640:800, 0:64], f[640:800, 64:128]))
        for f in (jnp.where(side, fa, fb), jnp.where(side, fb, fa))
    ]
    half = 0.5 * inv_ref[0:1, 0:1]
    corner_l = stack(lanes(corner_l, zeros(320, 1)), zeros(64, 6))
    corner_r = stack(zeros(64, 6), lanes(zeros(320, 1), corner_r))
    add_l = dot3(xh[320:640, 0:384], xl[320:640, 0:384], *split(corner_l))
    add_r = dot3(xh[384:704, 640:1024], xl[384:704, 640:1024], *split(corner_r))
    copies = []
    for i in range(6):
        at = slice(BS * i, BS * (i + 1))
        parts = []
        if i < 5:
            part = add_l[at, 64 * i : 320] * (half * ko_ref[i : i + 1, 64 * i : 320])
            parts.append(lanes(zeros(BS, 1), part))
        parts.append(zeros(BS, 12 - (6 - i if i < 5 else 0) - i))
        if i > 0:
            part = add_r[BS * (i - 1) : BS * i, 64 : 64 + 64 * i]
            parts.append(part * (half * ko_ref[i : i + 1, 704 : 704 + 64 * i]))
        out_ref[at, :] = part_ref[at, :] - lanes(*parts)
        copies.append(pltpu.make_async_copy(out_ref.at[at, :], out_hbm.at[at, :], sem.at[i]))
        copies[-1].start()
    for copy in copies:
        copy.wait()


def call(kernel, outs, args, flops, name, mib, scratch=(), in_hbm=(), out_hbm=()):
    args = [pltpu.with_memory_space_constraint(a, pltpu.HBM) if i in in_hbm else a for i, a in enumerate(args)]
    return pl.pallas_call(
        kernel,
        out_shape=[(pltpu.HBM if i in out_hbm else pltpu.VMEM)(s, t) for i, (s, t) in enumerate(outs)],
        in_specs=[HBM if i in in_hbm else VMEM for i in range(len(args))],
        out_specs=[HBM if i in out_hbm else VMEM for i in range(len(outs))],
        scratch_shapes=list(scratch),
        compiler_params=pltpu.CompilerParams(vmem_limit_bytes=mib << 20),
        cost_estimate=pl.CostEstimate(flops=flops, bytes_accessed=1 << 20, transcendentals=0),
        name=name,
    )(*args)


def local(hamiltonian, pattern):
    n_blk, n_rep = lax.axis_size("blk"), lax.axis_size("rep")
    size = math.sqrt(n_blk * n_rep * 6 * BS)
    band = hamiltonian.reshape(6 * BS, 12 * BS)
    own, corner, mask_o, mask_h, scalar = ((384, 1024), F32), ((320, 320), F32), ((8, 1024), F32), ((8, 640), F32), ((8, 128), F32)
    dma = pltpu.SemaphoreType.DMA((2,))
    wide, tall = pltpu.VMEM((1024, 1024), BF16), pltpu.VMEM((1024, 640), BF16)
    rows, far = pltpu.VMEM((384, 1024), BF16), pltpu.VMEM((336, 384), F32)

    m, mask, to_b, to_a, ssq = call(
        prepare_kernel,
        [((384, 768), F32), ((8, 768), F32), ((336, 384), F32), ((336, 384), F32), ((n_rep, 1, 128), F32)],
        (band, pattern), 10**7, "prepare", 16,
        scratch=[pltpu.VMEM((384, 768), F32), pltpu.VMEM((6, 12), jnp.int32), pltpu.VMEM((n_rep, 1, 128), F32), dma],
        in_hbm=(0, 1), out_hbm=(4,),
    )
    first_b, first_a = across(to_b), inside(to_a)
    ssq = lax.all_to_all(ssq, "rep", 0, 0)
    s, top = call(
        square_kernel, [own, scalar], (m, mask, first_b, first_a), 10**9, "first_square", 24,
        scratch=[rows, rows, wide, wide, far, far, dma], in_hbm=(2, 3),
    )
    to_b, to_a, top, ssq = call(
        send_kernel, [((192, 384), F32), ((192, 384), F32), scalar, ((n_blk, 1, 128), F32)],
        (ssq, s, top), 10**6, "send", 16, scratch=[pltpu.VMEM((n_blk, 1, 128), F32), dma], out_hbm=(3,),
    )
    from_b, from_a = across(to_b), inside(to_a)
    ssq = lax.all_to_all(ssq, "blk", 0, 0)
    s_l, s_r = call(
        halo_square_kernel, [corner, corner], (top, m, first_b, first_a), 10**9, "halo_square", 24,
        scratch=[far, far, pltpu.VMEM(*corner), pltpu.VMEM(*corner), dma], in_hbm=(2, 3), out_hbm=(0, 1),
    )
    x, xh, xl, s2, to_b, to_a, inverse, ko, kl, kr = call(
        lambda *refs: second_kernel(*refs, size=size),
        [own, ((1024, 1024), BF16), ((1024, 1024), BF16), ((384, 512), F32),
         ((800, 128), F32), ((800, 128), F32), scalar, mask_o, mask_h, mask_h],
        (ssq, top, m, mask, s, first_b, first_a, s_l, s_r, from_b, from_a), 10**10, "second_square", 32,
        scratch=[rows] * 2 + [tall] * 4 + [wide] * 2 + [far] * 2 + [pltpu.VMEM(*corner)] * 2
        + [pltpu.VMEM((192, 384), F32)] * 2 + [pltpu.SemaphoreType.DMA((6,))], in_hbm=(5, 6, 7, 8, 9, 10),
    )
    from_b, from_a = across(to_b), inside(to_a)
    (part,) = call(
        third_kernel, [((384, 768), F32)], (x, xh, xl, s2, ko, kl, kr, inverse), 5 * 10**9, "second_cubic", 24,
        scratch=[wide] * 2,
    )
    (out,) = call(
        last_kernel, [((384, 768), F32)], (part, xh, xl, ko, inverse, from_b, from_a), 10**9, "result", 16,
        scratch=[pltpu.VMEM((384, 768), F32), pltpu.SemaphoreType.DMA((6,))], out_hbm=(0,),
    )
    return out.reshape(6, BS, 12 * BS)


def solution(mesh):
    placed = (P(AXES, None, None), P(AXES, None))
    return jax.shard_map(
        local, mesh=mesh, in_specs=placed, out_specs=P(AXES, None, None), check_vma=False
    )
```

```python
import math

import jax
import jax.numpy as jnp
from jax import lax
from jax.experimental import pallas as pl
from jax.experimental.pallas import tpu as pltpu
from jax.sharding import PartitionSpec as P

BS = 64
AXES = ("blk", "rep")
F32 = jnp.float32
BF16 = jnp.bfloat16
VMEM = pl.BlockSpec(memory_space=pltpu.VMEM)
HBM = pl.BlockSpec(memory_space=pltpu.HBM)


def across(block):
    n = lax.axis_size(AXES)
    return lax.ppermute(block, AXES, [(i, (i + 1 if i % 2 else i - 1) % n) for i in range(n)])


def inside(block):
    n = lax.axis_size(AXES)
    return lax.ppermute(block, AXES, [(i, i ^ 1) for i in range(n)])


def odd():
    return lax.rem(lax.axis_index("rep"), 2) == 1


def zeros(rows, blocks):
    return jnp.zeros((rows, blocks * BS), F32)


def lanes(*parts):
    return jnp.concatenate([p for p in parts if p.shape[1]], axis=1)


def stack(*parts):
    return jnp.concatenate(parts, axis=0)


def split(x):
    high = x.astype(BF16)
    return high, (x - high.astype(F32)).astype(BF16)


def dot(a, b):
    return lax.dot_general(a, b, (((1,), (0,)), ((), ())), preferred_element_type=F32)


def dot3(a_high, a_low, b_high, b_low):
    return dot(a_high, b_high) + (dot(a_high, b_low) + dot(a_low, b_high))


def store(pair, start, value):
    for ref, part in zip(pair, split(value)):
        ref[start : start + value.shape[0], :] = part


def masked_rows(x, mask):
    return stack(*[x[BS * i : BS * (i + 1)] * mask[i : i + 1] for i in range(x.shape[0] // BS)])


def widen(x):
    return stack(*[lanes(zeros(128, 2 * p), x[128 * p : 128 * p + 128], zeros(128, 4 - 2 * p)) for p in range(3)])


def narrow(x):
    return stack(*[x[128 * p : 128 * p + 128, 128 * p : 128 * p + 768] for p in range(3)])


def own_product(left, right):
    out = []
    for p in range(3):
        rows, reach = slice(128 * p, 128 * p + 128), slice(128 * p, 128 * p + 768)
        out.append(dot3(left[0][rows, reach], left[1][rows, reach], right[0][reach, reach], right[1][reach, reach]))
    return widen(stack(*out))


def own_window(x):
    n = x.shape[0] // 6 if x.shape[0] > 8 else 1
    out = [lanes(x[0:n, BS:], zeros(n, 5))]
    for i in range(1, 6):
        out.append(lanes(zeros(n, i - 1), x[n * i : n * (i + 1)], zeros(n, 5 - i)))
    return stack(*out)


def mirror(a, lower):
    br = lax.broadcasted_iota(jnp.int32, a.shape, 0) // BS
    bc = lax.broadcasted_iota(jnp.int32, a.shape, 1) // BS
    keep = br >= bc if lower else br <= bc
    return jnp.where(keep, a, a.T)


def prepare_kernel(h_hbm, pat_hbm, m_ref, mask_ref, b_ref, a_ref, ssq_ref, h_ref, pat_ref, sem):
    fetch_pat = pltpu.make_async_copy(pat_hbm, pat_ref, sem.at[0])
    fetch_h = [
        pltpu.make_async_copy(h_hbm.at[BS * i : BS * (i + 1), :], h_ref.at[BS * i : BS * (i + 1), :], sem.at[1 + i])
        for i in range(6)
    ]
    fetch_pat.start()
    for copy in fetch_h:
        copy.start()
    fetch_pat.wait()
    pat = pat_ref[...].astype(F32)
    owner = lax.broadcasted_iota(jnp.int32, (12, 12 * BS), 1) // BS
    spread = (owner == lax.broadcasted_iota(jnp.int32, (12, 12 * BS), 0)).astype(F32)
    mask = stack(dot(pat, spread), jnp.zeros((2, 12 * BS), F32))
    mask_ref[...] = mask
    side = odd()
    for start, part in ((320, mask[:, 64:448]), (328, lanes(mask[:, 448:768], zeros(8, 1)))):
        b_ref[start : start + 8, :] = part
        a_ref[start : start + 8, :] = part
    total = jnp.zeros((8, 128), F32)
    rows = []
    for i in range(6):
        at = slice(BS * i, BS * (i + 1))
        fetch_h[i].wait()
        row = h_ref[at, :] * mask[i : i + 1, :]
        m_ref[at, :] = row
        square = row * row
        for a in range(8):
            for b in range(6):
                total = total + square[8 * a : 8 * a + 8, 128 * b : 128 * b + 128]
        rows.append(row)
    ssq_ref[...] = jnp.zeros(ssq_ref.shape, F32) + jnp.sum(total)
    for i in range(5):
        at = slice(BS * i, BS * (i + 1))
        to_right, to_left = rows[i + 1][:, 64:448], rows[i][:, 384:768]
        b_ref[at, :] = jnp.where(side, to_right, to_left)
        a_ref[at, :] = jnp.where(side, to_left, to_right)


def copy_all(sem, *pairs):
    copies = [pltpu.make_async_copy(source, target, sem.at[i]) for i, (source, target) in enumerate(pairs)]
    for copy in copies:
        copy.start()
    return copies


def halos(across_ref, inside_ref):
    side = odd()
    fb, fa = across_ref[...], inside_ref[...]
    return jnp.where(side, fa, fb), jnp.where(side, fb, fa)


def surroundings(own, fl, fr, g):
    fl, fr = fl[0:320] * g, fr[0:320] * g
    low = stack(*[lanes(zeros(BS, i), fl[BS * i : BS * (i + 1)], zeros(BS, 4 - i)) for i in range(5)])
    high = stack(*[lanes(zeros(BS, i), fr[BS * i : BS * (i + 1)], zeros(BS, 4 - i)) for i in range(5)])
    cross_l = own[:, 0:384].T[0:320]
    cross_r = own[:, 640:1024].T[64:384]
    hl = lanes(zeros(320, 1), low[:, 0:320], mirror(low[:, 320:640], True), cross_l[:, 0:320])
    hr = lanes(cross_r[:, 64:384], mirror(high[:, 0:320], False), high[:, 320:640], zeros(320, 1))
    return hl, hr


def masks(mask_own, fl, fr):
    mask_l, mask_r = [], []
    for i in range(5):
        band = lanes(fl[321 + i : 322 + i], fl[329 + i : 330 + i, 0:320])
        mask_l.append(lanes(zeros(1, 1 + i), band, zeros(1, 4 - i))[:, 384:1024])
        band = lanes(fr[320 + i : 321 + i], fr[328 + i : 329 + i, 0:320])
        mask_r.append(lanes(zeros(1, i), band, zeros(1, 5 - i))[:, 0:640])
    return own_window(mask_own), stack(*mask_l), stack(*mask_r)


def square_kernel(
    m_ref, mask_ref, b_ref, a_ref, ssq_ref,
    hl_hbm, hr_hbm, s_ref, ko_ref, kl_ref, kr_ref, top_ref, sb_ref, sa_ref, sum_ref,
    oh, ol, wh, wl, hl_ref, hr_ref, sem,
):
    sum_ref[...] = jnp.zeros(sum_ref.shape, F32) + jnp.sum(ssq_ref[...]) / 128.0
    fl, fr = halos(b_ref, a_ref)
    m = m_ref[...]
    top = jnp.maximum(jnp.max(jnp.abs(fl[0:320])), jnp.max(jnp.abs(fr[0:320])))
    top = jnp.maximum(jnp.maximum(top, jnp.max(jnp.abs(m))), 1e-11)
    top_ref[...] = jnp.zeros(top_ref.shape, F32) + top
    mask_o, mask_l, mask_r = masks(mask_ref[...], fl, fr)
    ko_ref[...] = stack(mask_o, jnp.zeros((2, 1024), F32))
    kl_ref[...] = stack(mask_l, jnp.zeros((3, 640), F32))
    kr_ref[...] = stack(mask_r, jnp.zeros((3, 640), F32))
    own = own_window(m) * (1.0 / top)
    hl, hr = surroundings(own, fl, fr, 1.0 / top)
    hl_ref[...] = hl
    hr_ref[...] = hr
    copies = copy_all(sem, (hl_ref, hl_hbm), (hr_ref, hr_hbm))
    store((oh, ol), 0, own)
    store((wh, wl), 0, lanes(hl[:, 384:1024], zeros(320, 6)))
    wh[320:704, :], wl[320:704, :] = oh[...], ol[...]
    store((wh, wl), 704, lanes(zeros(320, 6), hr[:, 0:640]))
    s = masked_rows(own_product((oh, ol), (wh, wl)), mask_o)
    s_ref[...] = narrow(s)
    side = odd()
    scale = zeros(BS, 3) + top
    row = [s[BS * i : BS * (i + 1)] for i in range(6)]
    to_right = stack(
        lanes(row[1][:, 64:384], row[5][:, 320:384]),
        lanes(row[2][:, 128:384], row[4][:, 256:384]),
        lanes(row[3][:, 192:384], scale),
    )
    to_left = stack(
        lanes(row[4][:, 640:960], row[0][:, 640:704]),
        lanes(row[3][:, 640:896], row[1][:, 640:768]),
        lanes(row[2][:, 640:832], scale),
    )
    sb_ref[...] = jnp.where(side, to_right, to_left)
    sa_ref[...] = jnp.where(side, to_left, to_right)
    for copy in copies:
        copy.wait()


def second_kernel(
    norms_ref, top_ref, s_ref, ko_ref, kl_ref, kr_ref, h_hbm, hl_hbm, hr_hbm,
    hl_ref, hr_ref, x_ref, xh, xl, s2_ref, sl_ref, sr_ref, b_ref, a_ref, scal_ref,
    oh, ol, wh, wl, h_ref, sem, *, size
):
    copies = copy_all(sem, (h_hbm, h_ref), (hl_hbm, hl_ref), (hr_hbm, hr_ref))
    s = widen(s_ref[...])
    store((wh, wl), 320, s)
    copies[0].wait()
    own = masked_rows(own_window(h_ref[...]), ko_ref[0:6, :] * (1.0 / top_ref[0:1, 0:1]))
    store((oh, ol), 0, own)
    copies[1].wait()
    hl = hl_ref[...]
    hl_h, hl_l = split(hl)
    far_h, far_l = split(lanes(hl[:, 0:384].T[64:384], zeros(320, 1)))
    none = jnp.zeros((64, 384), BF16)
    right_h = stack(none, far_h, hl_h[:, 384:768], oh[0:320, 0:384])
    right_l = stack(none, far_l, hl_l[:, 384:768], ol[0:320, 0:384])
    s_l = masked_rows(dot3(hl_h, hl_l, right_h, right_l)[:, 0:320], kl_ref[0:5, 0:320])
    sl_ref[...] = s_l
    copies[2].wait()
    hr = hr_ref[...]
    hr_h, hr_l = split(hr)
    far_h, far_l = split(lanes(zeros(320, 1), hr[:, 640:1024].T[0:320]))
    right_h = stack(oh[64:384, 640:1024], hr_h[:, 256:640], far_h, none)
    right_l = stack(ol[64:384, 640:1024], hr_l[:, 256:640], far_l, none)
    s_r = masked_rows(dot3(hr_h, hr_l, right_h, right_l)[:, 64:384], kr_ref[0:5, 320:640])
    sr_ref[...] = s_r

    store((wh, wl), 0, lanes(s_l, s[:, 0:384].T[0:320, 0:320], zeros(320, 6)))
    store((wh, wl), 704, lanes(zeros(320, 6), s[:, 640:1024].T[64:384, 64:384], s_r))
    t_o = masked_rows(own_product((oh, ol), (wh, wl)), ko_ref[0:6, :])
    t_l = dot3(hl_h[:, 384:1024], hl_l[:, 384:1024], wh[0:640, 256:640], wl[0:640, 256:640])
    t_l = masked_rows(t_l[:, 64:384], kl_ref[0:5, 320:640])
    t_r = dot3(hr_h[:, 0:640], hr_l[:, 0:640], wh[384:1024, 384:768], wl[384:1024, 384:768])
    t_r = masked_rows(t_r[:, 0:320], kr_ref[0:5, 0:320])

    frob = jnp.sqrt(jnp.sum(norms_ref[...], keepdims=True)[0] / 128.0)
    inverse = 3.0 * frob / size
    r = top_ref[0:1, 0:1] / inverse
    c1 = 1.5 * r
    c3 = 0.5 * r * r * r
    for i, value in enumerate((inverse, c1, c3)):
        scal_ref[8 * i : 8 * i + 8, :] = jnp.zeros((8, 128), F32) + value
    x = c1 * own - c3 * t_o
    x_ref[...] = x
    store((xh, xl), 0, lanes(zeros(320, 5), c1 * hl[:, 704:1024] - c3 * t_l, zeros(320, 6)))
    store((xh, xl), 320, x)
    store((xh, xl), 704, lanes(zeros(320, 6), c1 * hr[:, 0:320] - c3 * t_r, zeros(320, 5)))
    s2 = []
    for p in range(3):
        rows, reach = slice(320 + 128 * p, 448 + 128 * p), slice(128 * p, 128 * p + 768)
        s2.append(dot3(xh[rows, reach], xl[rows, reach], xh[reach, 256:768], xl[reach, 256:768]))
    s2 = masked_rows(stack(*s2), ko_ref[0:6, 256:768])[:, 64:448]
    s2_ref[...] = s2

    def pack(block):
        tail = lanes(block[0:160, 256:320], block[160:320, 256:320])
        return stack(block[:, 0:128], block[:, 128:256], tail)

    side = odd()
    to_right, to_left = pack(s2[64:384, 64:384]), pack(s2[0:320, 0:320])
    b_ref[...] = jnp.where(side, to_right, to_left)
    a_ref[...] = jnp.where(side, to_left, to_right)


def third_kernel(
    x_ref, xh, xl, s2_ref, hl_ref, hr_ref, s_ref, sl_ref, sr_ref, fb_ref, fa_ref, top_ref, scal_ref, ko_ref, kl_ref, kr_ref,
    out_ref, wh, wl
):
    top = top_ref[0:1, 0:1]
    inverse, c1, c3 = scal_ref[0:1, 0:1], scal_ref[8:9, 0:1], scal_ref[16:17, 0:1]
    fl, fr = halos(fb_ref, fa_ref)
    far_l = stack(
        fl[0:64, 0:320],
        lanes(zeros(BS, 1), fl[64:128, 0:256]),
        lanes(zeros(BS, 2), fl[128:192, 0:192]),
        lanes(zeros(BS, 3), fl[64:128, 256:384]),
        lanes(zeros(BS, 4), fl[0:64, 320:384]),
    )
    far_r = stack(
        lanes(fr[0:64, 320:384], zeros(BS, 4)),
        lanes(fr[64:128, 256:384], zeros(BS, 3)),
        lanes(fr[128:192, 0:192], zeros(BS, 2)),
        lanes(fr[64:128, 0:256], zeros(BS, 1)),
        fr[0:64, 0:320],
    )
    ratio_l, ratio_r = fl[128:129, 192:193] / top, fr[128:129, 192:193] / top
    hl, hr = hl_ref[...], hr_ref[...]
    s = widen(s_ref[...])
    right = stack(zeros(64, 5), (far_l * ratio_l * ratio_l).T, sl_ref[...], s[0:320, 0:320])
    t_l = masked_rows(dot3(*split(hl), *split(right)), kl_ref[0:5, 0:320])
    right = stack(s[64:384, 704:1024], sr_ref[...], (far_r * ratio_r * ratio_r).T, zeros(64, 5))
    t_r = masked_rows(dot3(*split(hr), *split(right)), kr_ref[0:5, 320:640])
    xl_h, xl_l = split(c1 * hl[:, 384:704] - c3 * t_l)
    xr_h, xr_l = split(c1 * hr[:, 320:640] - c3 * t_r)

    ah, al = xh[320:704, :], xl[320:704, :]
    right_h = stack(lanes(xl_h, xh[0:320, 320:384]), xh[320:704, 0:384])
    right_l = stack(lanes(xl_l, xl[0:320, 320:384]), xl[320:704, 0:384])
    s2_a = []
    for p in range(3):
        rows = slice(128 * p, 128 * p + 128)
        part = dot3(ah[rows, 0:704], al[rows, 0:704], right_h[:, 128 * p :], right_l[:, 128 * p :])
        s2_a.append(lanes(zeros(128, 2 * p), part))
    s2_a = masked_rows(stack(*s2_a), ko_ref[0:6, 0:384])
    right_h = stack(xh[320:704, 640:1024], lanes(xh[704:1024, 640:704], xr_h))
    right_l = stack(xl[320:704, 640:1024], lanes(xl[704:1024, 640:704], xr_l))
    s2_b = []
    for p in range(3):
        rows, end = slice(128 * p, 128 * p + 128), 128 * (p + 1)
        part = dot3(ah[rows, 320:1024], al[rows, 320:1024], right_h[:, 0:end], right_l[:, 0:end])
        s2_b.append(lanes(part, zeros(128, 4 - 2 * p)))
    s2_b = masked_rows(stack(*s2_b), ko_ref[0:6, 640:1024])
    left_h, left_l = lanes(xl_h, xh[0:320, 320:640]), lanes(xl_l, xl[0:320, 320:640])
    s2_l = dot3(left_h, left_l, xh[0:640, 256:640], xl[0:640, 256:640])
    s2_l = masked_rows(s2_l[:, 64:384], kl_ref[0:5, 320:640])
    left_h, left_l = lanes(xh[704:1024, 384:704], xr_h), lanes(xl[704:1024, 384:704], xr_l)
    s2_r = dot3(left_h, left_l, xh[384:1024, 384:768], xl[384:1024, 384:768])
    s2_r = masked_rows(s2_r[:, 0:320], kr_ref[0:5, 0:320])
    store((wh, wl), 0, lanes(zeros(320, 5), s2_l, zeros(320, 6)))
    store((wh, wl), 320, lanes(s2_a[:, 0:320], s2_ref[...], s2_b[:, 64:384]))
    store((wh, wl), 704, lanes(zeros(320, 6), s2_r, zeros(320, 5)))
    cubic = own_product((xh.at[320:704, :], xl.at[320:704, :]), (wh, wl))
    for i in range(6):
        at = slice(BS * i, BS * (i + 1))
        row = (1.5 * x_ref[at, :] - 0.5 * (cubic[at] * ko_ref[i : i + 1, :])) * inverse
        if i == 0:
            out_ref[at, :] = lanes(zeros(BS, 1), row[:, 0:704])
        else:
            out_ref[at, :] = row[:, 64 * (i - 1) : 64 * (i - 1) + 768]


def last_kernel(part_ref, xh, xl, ko_ref, scal_ref, fb_ref, fa_ref, out_hbm, out_ref, sem):
    corner_l, corner_r = [
        lanes(f[0:320], f[320:640], stack(f[640:800, 0:64], f[640:800, 64:128]))
        for f in halos(fb_ref, fa_ref)
    ]
    half = 0.5 * scal_ref[0:1, 0:1]
    corner_l = stack(lanes(corner_l, zeros(320, 1)), zeros(64, 6))
    corner_r = stack(zeros(64, 6), lanes(zeros(320, 1), corner_r))
    add_l = dot3(xh[320:640, 0:384], xl[320:640, 0:384], *split(corner_l))
    add_r = dot3(xh[384:704, 640:1024], xl[384:704, 640:1024], *split(corner_r))
    copies = []
    for i in range(6):
        at = slice(BS * i, BS * (i + 1))
        parts = []
        if i < 5:
            part = add_l[at, 64 * i : 320] * (half * ko_ref[i : i + 1, 64 * i : 320])
            parts.append(lanes(zeros(BS, 1), part))
        parts.append(zeros(BS, 12 - (6 - i if i < 5 else 0) - i))
        if i > 0:
            part = add_r[BS * (i - 1) : BS * i, 64 : 64 + 64 * i]
            parts.append(part * (half * ko_ref[i : i + 1, 704 : 704 + 64 * i]))
        out_ref[at, :] = part_ref[at, :] - lanes(*parts)
        copies.append(pltpu.make_async_copy(out_ref.at[at, :], out_hbm.at[at, :], sem.at[i]))
        copies[-1].start()
    for copy in copies:
        copy.wait()


def call(kernel, outs, args, flops, name, mib, scratch=(), in_hbm=(), out_hbm=()):
    args = [pltpu.with_memory_space_constraint(a, pltpu.HBM) if i in in_hbm else a for i, a in enumerate(args)]
    return pl.pallas_call(
        kernel,
        out_shape=[(pltpu.HBM if i in out_hbm else pltpu.VMEM)(s, t) for i, (s, t) in enumerate(outs)],
        in_specs=[HBM if i in in_hbm else VMEM for i in range(len(args))],
        out_specs=[HBM if i in out_hbm else VMEM for i in range(len(outs))],
        scratch_shapes=list(scratch),
        compiler_params=pltpu.CompilerParams(vmem_limit_bytes=mib << 20),
        cost_estimate=pl.CostEstimate(flops=flops, bytes_accessed=1 << 20, transcendentals=0),
        name=name,
    )(*args)


def local(hamiltonian, pattern):
    n_blk, n_rep = lax.axis_size("blk"), lax.axis_size("rep")
    size = math.sqrt(n_blk * n_rep * 6 * BS)
    band = hamiltonian.reshape(6 * BS, 12 * BS)
    own, halo, corner, full = ((384, 1024), F32), ((320, 1024), F32), ((320, 320), F32), ((1024, 1024), BF16)
    mask_o, mask_h, scalar = ((8, 1024), F32), ((8, 640), F32), ((8, 128), F32)
    rows, far = ((384, 1024), BF16), ((192, 384), F32)
    dma = pltpu.SemaphoreType.DMA((2,))

    m, mask, to_b, to_a, ssq = call(
        prepare_kernel,
        [((384, 768), F32), ((8, 768), F32), ((336, 384), F32), ((336, 384), F32), ((n_rep, 1, 128), F32)],
        (band, pattern), 10**7, "prepare", 16,
        scratch=[pltpu.VMEM((384, 768), F32), pltpu.VMEM((6, 12), jnp.int32), pltpu.SemaphoreType.DMA((7,))],
        in_hbm=(0, 1),
    )
    first_b, first_a = across(to_b), inside(to_a)
    ssq = lax.all_to_all(ssq, "rep", 0, 0)
    wide = pltpu.VMEM((1024, 1024), BF16)
    scratch = [pltpu.VMEM(*rows)] * 2 + [wide] * 2
    hl, hr, s, ko, kl, kr, top, to_b, to_a, ssq = call(
        square_kernel,
        [halo, halo, ((384, 768), F32), mask_o, mask_h, mask_h, scalar, far, far, ((n_blk, 1, 128), F32)],
        (m, mask, first_b, first_a, ssq), 10**9, "first_square", 20,
        scratch=scratch + [pltpu.VMEM(*halo), pltpu.VMEM(*halo), dma], out_hbm=(0, 1),
    )
    far_b, far_a = across(to_b), inside(to_a)
    ssq = lax.all_to_all(ssq, "blk", 0, 0)
    hl, hr, x, xh, xl, s2, s_l, s_r, to_b, to_a, scalars = call(
        lambda *refs: second_kernel(*refs, size=size),
        [halo, halo, own, full, full, ((384, 384), F32), corner, corner, ((800, 128), F32), ((800, 128), F32),
         ((24, 128), F32)],
        (ssq, top, s, ko, kl, kr, band, hl, hr), 10**10, "second_square", 24,
        scratch=scratch + [pltpu.VMEM((384, 768), F32), pltpu.SemaphoreType.DMA((3,))], in_hbm=(6, 7, 8),
    )
    from_b, from_a = across(to_b), inside(to_a)
    (part,) = call(
        third_kernel, [((384, 768), F32)],
        (x, xh, xl, s2, hl, hr, s, s_l, s_r, far_b, far_a, top, scalars, ko, kl, kr),
        5 * 10**9, "second_cubic", 24, scratch=[wide, wide],
    )
    (out,) = call(
        last_kernel, [((384, 768), F32)], (part, xh, xl, ko, scalars, from_b, from_a), 10**9, "result", 16,
        scratch=[pltpu.VMEM((384, 768), F32), pltpu.SemaphoreType.DMA((6,))], out_hbm=(0,),
    )
    return out.reshape(6, BS, 12 * BS)


def solution(mesh):
    placed = (P(AXES, None, None), P(AXES, None))
    return jax.shard_map(
        local, mesh=mesh, in_specs=placed, out_specs=P(AXES, None, None), check_vma=False
    )
```

```python
import math

import jax
import jax.numpy as jnp
from jax import lax
from jax.experimental import pallas as pl
from jax.experimental.pallas import tpu as pltpu
from jax.sharding import PartitionSpec as P

BS = 64
AXES = ("blk", "rep")
F32 = jnp.float32
BF16 = jnp.bfloat16
VMEM = pl.BlockSpec(memory_space=pltpu.VMEM)
HBM = pl.BlockSpec(memory_space=pltpu.HBM)


def across(block):
    n = lax.axis_size(AXES)
    return lax.ppermute(block, AXES, [(i, (i + 1 if i % 2 else i - 1) % n) for i in range(n)])


def inside(block):
    n = lax.axis_size(AXES)
    return lax.ppermute(block, AXES, [(i, i ^ 1) for i in range(n)])


def odd():
    return lax.rem(lax.axis_index("rep"), 2) == 1


def zeros(rows, blocks):
    return jnp.zeros((rows, blocks * BS), F32)


def lanes(*parts):
    return jnp.concatenate([p for p in parts if p.shape[1]], axis=1)


def stack(*parts):
    return jnp.concatenate(parts, axis=0)


def split(x):
    high = x.astype(BF16)
    return high, (x - high.astype(F32)).astype(BF16)


def dot(a, b):
    return lax.dot_general(a, b, (((1,), (0,)), ((), ())), preferred_element_type=F32)


def dot3(a_high, a_low, b_high, b_low):
    return dot(a_high, b_high) + (dot(a_high, b_low) + dot(a_low, b_high))


def cross_left(left, right):
    (lh, ll), (rh, rl) = left, right
    upper = dot3(lh[0:192, 0:512], ll[0:192, 0:512], rh[0:512, 256:512], rl[0:512, 256:512])
    lower = dot3(lh[192:320, :], ll[192:320, :], rh[0:640, 256:640], rl[0:640, 256:640])
    return stack(lanes(upper[:, 64:256], zeros(192, 2)), lower[:, 64:384])


def cross_right(left, right):
    (lh, ll), (rh, rl) = left, right
    upper = dot3(lh[0:128, :], ll[0:128, :], rh[384:1024, 384:768], rl[384:1024, 384:768])
    lower = dot3(lh[128:320, 128:640], ll[128:320, 128:640], rh[512:1024, 512:768], rl[512:1024, 512:768])
    return stack(upper[:, 0:320], lanes(zeros(192, 2), lower[:, 0:192]))


def gram(high, low):
    def times(a, b):
        return lax.dot_general(a, b, (((1,), (1,)), ((), ())), preferred_element_type=F32)

    mixed = times(high, low)
    return times(high, high) + (mixed + mixed.T)


def store(pair, start, value):
    for ref, part in zip(pair, split(value)):
        ref[start : start + value.shape[0], :] = part


def masked_rows(x, mask):
    return stack(*[x[BS * i : BS * (i + 1)] * mask[i : i + 1] for i in range(x.shape[0] // BS)])


def widen(x):
    return stack(*[lanes(zeros(128, 2 * p), x[128 * p : 128 * p + 128], zeros(128, 4 - 2 * p)) for p in range(3)])


def narrow(x):
    return stack(*[x[128 * p : 128 * p + 128, 128 * p : 128 * p + 768] for p in range(3)])


def own_product(left, right):
    out = []
    for p in range(3):
        rows, reach = slice(128 * p, 128 * p + 128), slice(128 * p, 128 * p + 768)
        out.append(dot3(left[0][rows, reach], left[1][rows, reach], right[0][reach, reach], right[1][reach, reach]))
    return widen(stack(*out))


def own_window(x):
    n = x.shape[0] // 6 if x.shape[0] > 8 else 1
    out = [lanes(x[0:n, BS:], zeros(n, 5))]
    for i in range(1, 6):
        out.append(lanes(zeros(n, i - 1), x[n * i : n * (i + 1)], zeros(n, 5 - i)))
    return stack(*out)


def mirror(a, lower):
    br = lax.broadcasted_iota(jnp.int32, a.shape, 0) // BS
    bc = lax.broadcasted_iota(jnp.int32, a.shape, 1) // BS
    keep = br >= bc if lower else br <= bc
    return jnp.where(keep, a, a.T)


def prepare_kernel(h_hbm, pat_hbm, m_ref, mask_ref, b_ref, a_ref, ssq_ref, h_ref, pat_ref, sem):
    fetch_pat = pltpu.make_async_copy(pat_hbm, pat_ref, sem.at[0])
    fetch_h = [
        pltpu.make_async_copy(h_hbm.at[BS * i : BS * (i + 1), :], h_ref.at[BS * i : BS * (i + 1), :], sem.at[1 + i])
        for i in range(6)
    ]
    fetch_pat.start()
    for copy in fetch_h:
        copy.start()
    fetch_pat.wait()
    pat = pat_ref[...].astype(F32)
    owner = lax.broadcasted_iota(jnp.int32, (12, 12 * BS), 1) // BS
    spread = (owner == lax.broadcasted_iota(jnp.int32, (12, 12 * BS), 0)).astype(F32)
    mask = stack(dot(pat, spread), jnp.zeros((2, 12 * BS), F32))
    mask_ref[...] = mask
    side = odd()
    for start, part in ((320, mask[:, 64:448]), (328, lanes(mask[:, 448:768], zeros(8, 1)))):
        b_ref[start : start + 8, :] = part
        a_ref[start : start + 8, :] = part
    total = jnp.zeros((8, 128), F32)
    rows = []
    for i in range(6):
        at = slice(BS * i, BS * (i + 1))
        fetch_h[i].wait()
        row = h_ref[at, :] * mask[i : i + 1, :]
        m_ref[at, :] = row
        square = row * row
        for a in range(8):
            for b in range(6):
                total = total + square[8 * a : 8 * a + 8, 128 * b : 128 * b + 128]
        rows.append(row)
    ssq_ref[...] = jnp.zeros(ssq_ref.shape, F32) + jnp.sum(total)
    for i in range(5):
        at = slice(BS * i, BS * (i + 1))
        to_right, to_left = rows[i + 1][:, 64:448], rows[i][:, 384:768]
        b_ref[at, :] = jnp.where(side, to_right, to_left)
        a_ref[at, :] = jnp.where(side, to_left, to_right)


def copy_all(sem, *pairs):
    copies = [pltpu.make_async_copy(source, target, sem.at[i]) for i, (source, target) in enumerate(pairs)]
    for copy in copies:
        copy.start()
    return copies


def halos(across_ref, inside_ref):
    side = odd()
    fb, fa = across_ref[...], inside_ref[...]
    return jnp.where(side, fa, fb), jnp.where(side, fb, fa)


def surroundings(own, fl, fr, g):
    fl, fr = fl[0:320] * g, fr[0:320] * g
    low = stack(*[lanes(zeros(BS, i), fl[BS * i : BS * (i + 1)], zeros(BS, 4 - i)) for i in range(5)])
    high = stack(*[lanes(zeros(BS, i), fr[BS * i : BS * (i + 1)], zeros(BS, 4 - i)) for i in range(5)])
    cross_l = own[:, 0:384].T[0:320]
    cross_r = own[:, 640:1024].T[64:384]
    hl = lanes(zeros(320, 1), low[:, 0:320], mirror(low[:, 320:640], True), cross_l[:, 0:320])
    hr = lanes(cross_r[:, 64:384], mirror(high[:, 0:320], False), high[:, 320:640], zeros(320, 1))
    return hl, hr


def masks(mask_own, fl, fr):
    mask_l, mask_r = [], []
    for i in range(5):
        band = lanes(fl[321 + i : 322 + i], fl[329 + i : 330 + i, 0:320])
        mask_l.append(lanes(zeros(1, 1 + i), band, zeros(1, 4 - i))[:, 384:1024])
        band = lanes(fr[320 + i : 321 + i], fr[328 + i : 329 + i, 0:320])
        mask_r.append(lanes(zeros(1, i), band, zeros(1, 5 - i))[:, 0:640])
    return own_window(mask_own), stack(*mask_l), stack(*mask_r)


def square_kernel(
    m_ref, mask_ref, b_ref, a_ref, ssq_ref,
    hl_hbm, hr_hbm, s_ref, ko_ref, kl_ref, kr_ref, top_ref, sb_ref, sa_ref, sum_ref,
    oh, ol, wh, wl, hl_ref, hr_ref, sem,
):
    sum_ref[...] = jnp.zeros(sum_ref.shape, F32) + jnp.sum(ssq_ref[...]) / 128.0
    fl, fr = halos(b_ref, a_ref)
    m = m_ref[...]
    top = jnp.maximum(jnp.max(jnp.abs(fl[0:320])), jnp.max(jnp.abs(fr[0:320])))
    top = jnp.maximum(jnp.maximum(top, jnp.max(jnp.abs(m))), 1e-11)
    top_ref[...] = jnp.zeros(top_ref.shape, F32) + top
    mask_o, mask_l, mask_r = masks(mask_ref[...], fl, fr)
    ko_ref[...] = stack(mask_o, jnp.zeros((2, 1024), F32))
    kl_ref[...] = stack(mask_l, jnp.zeros((3, 640), F32))
    kr_ref[...] = stack(mask_r, jnp.zeros((3, 640), F32))
    own = own_window(m) * (1.0 / top)
    hl, hr = surroundings(own, fl, fr, 1.0 / top)
    hl_ref[...] = hl
    hr_ref[...] = hr
    copies = copy_all(sem, (hl_ref, hl_hbm), (hr_ref, hr_hbm))
    store((oh, ol), 0, own)
    store((wh, wl), 0, lanes(hl[:, 384:1024], zeros(320, 6)))
    wh[320:704, :], wl[320:704, :] = oh[...], ol[...]
    store((wh, wl), 704, lanes(zeros(320, 6), hr[:, 0:640]))
    s = masked_rows(own_product((oh, ol), (wh, wl)), mask_o)
    s_ref[...] = narrow(s)
    side = odd()
    scale = zeros(BS, 3) + top
    row = [s[BS * i : BS * (i + 1)] for i in range(6)]
    to_right = stack(
        lanes(row[1][:, 64:384], row[5][:, 320:384]),
        lanes(row[2][:, 128:384], row[4][:, 256:384]),
        lanes(row[3][:, 192:384], scale),
    )
    to_left = stack(
        lanes(row[4][:, 640:960], row[0][:, 640:704]),
        lanes(row[3][:, 640:896], row[1][:, 640:768]),
        lanes(row[2][:, 640:832], scale),
    )
    sb_ref[...] = jnp.where(side, to_right, to_left)
    sa_ref[...] = jnp.where(side, to_left, to_right)
    for copy in copies:
        copy.wait()


def second_kernel(
    norms_ref, top_ref, s_ref, ko_ref, kl_ref, kr_ref, h_hbm, hl_hbm, hr_hbm,
    hl_h, hl_l, hr_h, hr_l, wh, wl, near_l, near_r, x_ref, xh, xl, s2_ref, b_ref, a_ref, scal_ref,
    oh, ol, hl_ref, hr_ref, h_ref, sem, *, size
):
    copies = copy_all(sem, (h_hbm, h_ref), (hl_hbm, hl_ref), (hr_hbm, hr_ref))
    s = widen(s_ref[...])
    store((wh, wl), 320, s)
    copies[0].wait()
    own = masked_rows(own_window(h_ref[...]), ko_ref[0:6, :] * (1.0 / top_ref[0:1, 0:1]))
    store((oh, ol), 0, own)
    copies[1].wait()
    hl = hl_ref[...]
    store((hl_h, hl_l), 0, hl)
    s_l = masked_rows(gram(hl_h[...], hl_l[...]), kl_ref[0:5, 0:320])
    copies[2].wait()
    hr = hr_ref[...]
    store((hr_h, hr_l), 0, hr)
    s_r = masked_rows(gram(hr_h[...], hr_l[...]), kr_ref[0:5, 320:640])

    store((wh, wl), 0, lanes(s_l, s[:, 0:384].T[0:320, 0:320], zeros(320, 6)))
    store((wh, wl), 704, lanes(zeros(320, 6), s[:, 640:1024].T[64:384, 64:384], s_r))
    t_o = masked_rows(own_product((oh, ol), (wh, wl)), ko_ref[0:6, :])
    near_l[...] = hl[:, 384:704]
    near_r[...] = hr[:, 320:640]
    t_l = cross_left((hl_h[:, 384:1024], hl_l[:, 384:1024]), (wh, wl))
    t_l = masked_rows(t_l, kl_ref[0:5, 320:640])
    t_r = cross_right((hr_h[:, 0:640], hr_l[:, 0:640]), (wh, wl))
    t_r = masked_rows(t_r, kr_ref[0:5, 0:320])

    frob = jnp.sqrt(jnp.sum(norms_ref[...], keepdims=True)[0] / 128.0)
    inverse = 3.0 * frob / size
    r = top_ref[0:1, 0:1] / inverse
    c1 = 1.5 * r
    c3 = 0.5 * r * r * r
    for i, value in enumerate((inverse, c1, c3)):
        scal_ref[8 * i : 8 * i + 8, :] = jnp.zeros((8, 128), F32) + value
    x = c1 * own - c3 * t_o
    x_ref[...] = x
    store((xh, xl), 0, lanes(zeros(320, 5), c1 * hl[:, 704:1024] - c3 * t_l, zeros(320, 6)))
    store((xh, xl), 320, x)
    store((xh, xl), 704, lanes(zeros(320, 6), c1 * hr[:, 0:320] - c3 * t_r, zeros(320, 5)))
    s2 = []
    for p in range(3):
        rows, reach = slice(320 + 128 * p, 448 + 128 * p), slice(128 * p, 128 * p + 768)
        s2.append(dot3(xh[rows, reach], xl[rows, reach], xh[reach, 256:768], xl[reach, 256:768]))
    s2 = masked_rows(stack(*s2), ko_ref[0:6, 256:768])[:, 64:448]
    s2_ref[...] = s2

    def pack(block):
        tail = lanes(block[0:160, 256:320], block[160:320, 256:320])
        return stack(block[:, 0:128], block[:, 128:256], tail)

    side = odd()
    to_right, to_left = pack(s2[64:384, 64:384]), pack(s2[0:320, 0:320])
    b_ref[...] = jnp.where(side, to_right, to_left)
    a_ref[...] = jnp.where(side, to_left, to_right)


def third_kernel(
    x_ref, xh, xl, s2_ref, hl_h, hl_l, hr_h, hr_l, sh, sl, near_l, near_r, fb_ref, fa_ref, top_ref, scal_ref,
    ko_ref, kl_ref, kr_ref, out_ref, wh, wl
):
    top = top_ref[0:1, 0:1]
    inverse, c1, c3 = scal_ref[0:1, 0:1], scal_ref[8:9, 0:1], scal_ref[16:17, 0:1]
    fl, fr = halos(fb_ref, fa_ref)
    far_l = stack(
        fl[0:64, 0:320],
        lanes(zeros(BS, 1), fl[64:128, 0:256]),
        lanes(zeros(BS, 2), fl[128:192, 0:192]),
        lanes(zeros(BS, 3), fl[64:128, 256:384]),
        lanes(zeros(BS, 4), fl[0:64, 320:384]),
    )
    far_r = stack(
        lanes(fr[0:64, 320:384], zeros(BS, 4)),
        lanes(fr[64:128, 256:384], zeros(BS, 3)),
        lanes(fr[128:192, 0:192], zeros(BS, 2)),
        lanes(fr[64:128, 0:256], zeros(BS, 1)),
        fr[0:64, 0:320],
    )
    ratio_l, ratio_r = fl[128:129, 192:193] / top, fr[128:129, 192:193] / top
    far_h, far_s = split(stack(zeros(64, 6), lanes((far_l * ratio_l * ratio_l).T, zeros(320, 1))))
    right_h, right_l = stack(far_h, sh[0:640, 0:384]), stack(far_s, sl[0:640, 0:384])
    t_l = dot3(hl_h[...], hl_l[...], right_h, right_l)[:, 0:320]
    far_h, far_s = split(stack(lanes(zeros(320, 1), (far_r * ratio_r * ratio_r).T), zeros(64, 6)))
    right_h, right_l = stack(sh[384:1024, 640:1024], far_h), stack(sl[384:1024, 640:1024], far_s)
    t_r = dot3(hr_h[...], hr_l[...], right_h, right_l)[:, 64:384]
    xl_h, xl_l = split(c1 * near_l[...] - c3 * masked_rows(t_l, kl_ref[0:5, 0:320]))
    xr_h, xr_l = split(c1 * near_r[...] - c3 * masked_rows(t_r, kr_ref[0:5, 320:640]))

    ah, al = xh[320:704, :], xl[320:704, :]
    right_h = stack(lanes(xl_h, xh[0:320, 320:384]), xh[320:704, 0:384])
    right_l = stack(lanes(xl_l, xl[0:320, 320:384]), xl[320:704, 0:384])
    s2_a = []
    for p in range(3):
        rows, reach = slice(128 * p, 128 * p + 128), slice(128 * p, 640)
        part = dot3(ah[rows, reach], al[rows, reach], right_h[reach, 128 * p :], right_l[reach, 128 * p :])
        s2_a.append(lanes(zeros(128, 2 * p), part))
    s2_a = masked_rows(stack(*s2_a), ko_ref[0:6, 0:384])
    right_h = stack(xh[320:704, 640:1024], lanes(xh[704:1024, 640:704], xr_h))
    right_l = stack(xl[320:704, 640:1024], lanes(xl[704:1024, 640:704], xr_l))
    s2_b = []
    for p in range(3):
        rows, reach, end = slice(128 * p, 128 * p + 128), slice(384, 768 + 128 * p), 128 * (p + 1)
        inner = slice(64, 448 + 128 * p)
        part = dot3(ah[rows, reach], al[rows, reach], right_h[inner, 0:end], right_l[inner, 0:end])
        s2_b.append(lanes(part, zeros(128, 4 - 2 * p)))
    s2_b = masked_rows(stack(*s2_b), ko_ref[0:6, 640:1024])
    left_h, left_l = lanes(xl_h, xh[0:320, 320:640]), lanes(xl_l, xl[0:320, 320:640])
    s2_l = masked_rows(cross_left((left_h, left_l), (xh, xl)), kl_ref[0:5, 320:640])
    left_h, left_l = lanes(xh[704:1024, 384:704], xr_h), lanes(xl[704:1024, 384:704], xr_l)
    s2_r = masked_rows(cross_right((left_h, left_l), (xh, xl)), kr_ref[0:5, 0:320])
    store((wh, wl), 0, lanes(zeros(320, 5), s2_l, zeros(320, 6)))
    store((wh, wl), 320, lanes(s2_a[:, 0:320], s2_ref[...], s2_b[:, 64:384]))
    store((wh, wl), 704, lanes(zeros(320, 6), s2_r, zeros(320, 5)))
    cubic = own_product((xh.at[320:704, :], xl.at[320:704, :]), (wh, wl))
    for i in range(6):
        at = slice(BS * i, BS * (i + 1))
        row = (1.5 * x_ref[at, :] - 0.5 * (cubic[at] * ko_ref[i : i + 1, :])) * inverse
        if i == 0:
            out_ref[at, :] = lanes(zeros(BS, 1), row[:, 0:704])
        else:
            out_ref[at, :] = row[:, 64 * (i - 1) : 64 * (i - 1) + 768]


def last_kernel(part_ref, xh, xl, ko_ref, scal_ref, fb_ref, fa_ref, out_hbm, out_ref, sem):
    corner_l, corner_r = [
        lanes(f[0:320], f[320:640], stack(f[640:800, 0:64], f[640:800, 64:128]))
        for f in halos(fb_ref, fa_ref)
    ]
    half = 0.5 * scal_ref[0:1, 0:1]
    corner_l = stack(lanes(corner_l, zeros(320, 1)), zeros(64, 6))
    corner_r = stack(zeros(64, 6), lanes(zeros(320, 1), corner_r))
    ch, cl = split(corner_l)
    near = dot3(xh[448:640, 128:384], xl[448:640, 128:384], ch[128:384, 128:384], cl[128:384, 128:384])
    add_l = stack(dot3(xh[320:448, 0:384], xl[320:448, 0:384], ch, cl), lanes(zeros(192, 2), near))
    ch, cl = split(corner_r)
    near = dot3(xh[384:576, 640:896], xl[384:576, 640:896], ch[0:256, 0:256], cl[0:256, 0:256])
    add_r = stack(lanes(near, zeros(192, 2)), dot3(xh[576:704, 640:1024], xl[576:704, 640:1024], ch, cl))
    copies = []
    for i in range(6):
        at = slice(BS * i, BS * (i + 1))
        parts = []
        if i < 5:
            part = add_l[at, 64 * i : 320] * (half * ko_ref[i : i + 1, 64 * i : 320])
            parts.append(lanes(zeros(BS, 1), part))
        parts.append(zeros(BS, 12 - (6 - i if i < 5 else 0) - i))
        if i > 0:
            part = add_r[BS * (i - 1) : BS * i, 64 : 64 + 64 * i]
            parts.append(part * (half * ko_ref[i : i + 1, 704 : 704 + 64 * i]))
        out_ref[at, :] = part_ref[at, :] - lanes(*parts)
        copies.append(pltpu.make_async_copy(out_ref.at[at, :], out_hbm.at[at, :], sem.at[i]))
        copies[-1].start()
    for copy in copies:
        copy.wait()


def call(kernel, outs, args, flops, name, mib, scratch=(), in_hbm=(), out_hbm=()):
    args = [pltpu.with_memory_space_constraint(a, pltpu.HBM) if i in in_hbm else a for i, a in enumerate(args)]
    return pl.pallas_call(
        kernel,
        out_shape=[(pltpu.HBM if i in out_hbm else pltpu.VMEM)(s, t) for i, (s, t) in enumerate(outs)],
        in_specs=[HBM if i in in_hbm else VMEM for i in range(len(args))],
        out_specs=[HBM if i in out_hbm else VMEM for i in range(len(outs))],
        scratch_shapes=list(scratch),
        compiler_params=pltpu.CompilerParams(vmem_limit_bytes=mib << 20),
        cost_estimate=pl.CostEstimate(flops=flops, bytes_accessed=1 << 20, transcendentals=0),
        name=name,
    )(*args)


def local(hamiltonian, pattern):
    n_blk, n_rep = lax.axis_size("blk"), lax.axis_size("rep")
    size = math.sqrt(n_blk * n_rep * 6 * BS)
    band = hamiltonian.reshape(6 * BS, 12 * BS)
    own, halo, corner, full = ((384, 1024), F32), ((320, 1024), F32), ((320, 320), F32), ((1024, 1024), BF16)
    mask_o, mask_h, scalar = ((8, 1024), F32), ((8, 640), F32), ((8, 128), F32)
    rows, far = ((384, 1024), BF16), ((192, 384), F32)
    dma = pltpu.SemaphoreType.DMA((2,))

    m, mask, to_b, to_a, ssq = call(
        prepare_kernel,
        [((384, 768), F32), ((8, 768), F32), ((336, 384), F32), ((336, 384), F32), ((n_rep, 1, 128), F32)],
        (band, pattern), 10**7, "prepare", 16,
        scratch=[pltpu.VMEM((384, 768), F32), pltpu.VMEM((6, 12), jnp.int32), pltpu.SemaphoreType.DMA((7,))],
        in_hbm=(0, 1),
    )
    first_b, first_a = across(to_b), inside(to_a)
    ssq = lax.all_to_all(ssq, "rep", 0, 0)
    wide = pltpu.VMEM((1024, 1024), BF16)
    hl, hr, s, ko, kl, kr, top, to_b, to_a, ssq = call(
        square_kernel,
        [halo, halo, ((384, 768), F32), mask_o, mask_h, mask_h, scalar, far, far, ((n_blk, 1, 128), F32)],
        (m, mask, first_b, first_a, ssq), 10**9, "first_square", 20,
        scratch=[pltpu.VMEM(*rows)] * 2 + [wide] * 2 + [pltpu.VMEM(*halo), pltpu.VMEM(*halo), dma], out_hbm=(0, 1),
    )
    far_b, far_a = across(to_b), inside(to_a)
    ssq = lax.all_to_all(ssq, "blk", 0, 0)
    pair = ((320, 1024), BF16)
    *operands, x, xh, xl, s2, to_b, to_a, scalars = call(
        lambda *refs: second_kernel(*refs, size=size),
        [pair, pair, pair, pair, full, full, corner, corner, own, full, full, ((384, 384), F32),
         ((800, 128), F32), ((800, 128), F32), ((24, 128), F32)],
        (ssq, top, s, ko, kl, kr, band, hl, hr), 10**10, "second_square", 24,
        scratch=[pltpu.VMEM(*rows)] * 2 + [pltpu.VMEM(*halo)] * 2
        + [pltpu.VMEM((384, 768), F32), pltpu.SemaphoreType.DMA((3,))],
        in_hbm=(6, 7, 8),
    )
    from_b, from_a = across(to_b), inside(to_a)
    (part,) = call(
        third_kernel, [((384, 768), F32)],
        (x, xh, xl, s2, *operands, far_b, far_a, top, scalars, ko, kl, kr),
        5 * 10**9, "second_cubic", 24, scratch=[wide, wide],
    )
    (out,) = call(
        last_kernel, [((384, 768), F32)], (part, xh, xl, ko, scalars, from_b, from_a), 10**9, "result", 16,
        scratch=[pltpu.VMEM((384, 768), F32), pltpu.SemaphoreType.DMA((6,))], out_hbm=(0,),
    )
    return out.reshape(6, BS, 12 * BS)


def solution(mesh):
    placed = (P(AXES, None, None), P(AXES, None))
    return jax.shard_map(
        local, mesh=mesh, in_specs=placed, out_specs=P(AXES, None, None), check_vma=False
    )
```

```python
import math

import jax
import jax.numpy as jnp
from jax import lax
from jax.experimental import pallas as pl
from jax.experimental.pallas import tpu as pltpu
from jax.sharding import PartitionSpec as P

BS = 64
AXES = ("blk", "rep")
F32 = jnp.float32
BF16 = jnp.bfloat16
VMEM = pl.BlockSpec(memory_space=pltpu.VMEM)
HBM = pl.BlockSpec(memory_space=pltpu.HBM)


def across(block):
    n = lax.axis_size(AXES)
    return lax.ppermute(block, AXES, [(i, (i + 1 if i % 2 else i - 1) % n) for i in range(n)])


def inside(block):
    n = lax.axis_size(AXES)
    return lax.ppermute(block, AXES, [(i, i ^ 1) for i in range(n)])


def odd():
    return lax.rem(lax.axis_index("rep"), 2) == 1


def zeros(rows, blocks):
    return jnp.zeros((rows, blocks * BS), F32)


def lanes(*parts):
    return jnp.concatenate([p for p in parts if p.shape[1]], axis=1)


def stack(*parts):
    return jnp.concatenate(parts, axis=0)


def split(x):
    high = x.astype(BF16)
    return high, (x - high.astype(F32)).astype(BF16)


def dot(a, b):
    return lax.dot_general(a, b, (((1,), (0,)), ((), ())), preferred_element_type=F32)


def dot3(a_high, a_low, b_high, b_low):
    return dot(a_high, b_high) + (dot(a_high, b_low) + dot(a_low, b_high))


def cross_left(left, right):
    (lh, ll), (rh, rl) = left, right
    upper = dot3(lh[0:192, 0:512], ll[0:192, 0:512], rh[0:512, 256:512], rl[0:512, 256:512])
    lower = dot3(lh[192:320, :], ll[192:320, :], rh[0:640, 256:640], rl[0:640, 256:640])
    return stack(lanes(upper[:, 64:256], zeros(192, 2)), lower[:, 64:384])


def cross_right(left, right):
    (lh, ll), (rh, rl) = left, right
    upper = dot3(lh[0:128, :], ll[0:128, :], rh[384:1024, 384:768], rl[384:1024, 384:768])
    lower = dot3(lh[128:320, 128:640], ll[128:320, 128:640], rh[512:1024, 512:768], rl[512:1024, 512:768])
    return stack(upper[:, 0:320], lanes(zeros(192, 2), lower[:, 0:192]))


def gram(high, low):
    def times(a, b):
        return lax.dot_general(a, b, (((1,), (1,)), ((), ())), preferred_element_type=F32)

    mixed = times(high, low)
    return times(high, high) + (mixed + mixed.T)


def store(pair, start, value):
    for at in range(0, value.shape[0], 32):
        for ref, part in zip(pair, split(value[at : at + 32])):
            ref[start + at : start + at + 32, :] = part


def masked_rows(x, mask):
    return stack(*[x[BS * i : BS * (i + 1)] * mask[i : i + 1] for i in range(x.shape[0] // BS)])


def widen(x):
    return stack(*[lanes(zeros(128, 2 * p), x[128 * p : 128 * p + 128], zeros(128, 4 - 2 * p)) for p in range(3)])


def narrow(x):
    return stack(*[x[128 * p : 128 * p + 128, 128 * p : 128 * p + 768] for p in range(3)])


def own_product(left, right):
    out = []
    for p in range(3):
        rows, reach = slice(128 * p, 128 * p + 128), slice(128 * p, 128 * p + 768)
        out.append(dot3(left[0][rows, reach], left[1][rows, reach], right[0][reach, reach], right[1][reach, reach]))
    return widen(stack(*out))


def own_window(x):
    n = x.shape[0] // 6 if x.shape[0] > 8 else 1
    out = [lanes(x[0:n, BS:], zeros(n, 5))]
    for i in range(1, 6):
        out.append(lanes(zeros(n, i - 1), x[n * i : n * (i + 1)], zeros(n, 5 - i)))
    return stack(*out)


def mirror(a, lower):
    br = lax.broadcasted_iota(jnp.int32, a.shape, 0) // BS
    bc = lax.broadcasted_iota(jnp.int32, a.shape, 1) // BS
    keep = br >= bc if lower else br <= bc
    return jnp.where(keep, a, a.T)


def prepare_kernel(h_hbm, pat_hbm, m_ref, mask_ref, b_ref, a_ref, ssq_ref, h_ref, pat_ref, sem):
    fetch_pat = pltpu.make_async_copy(pat_hbm, pat_ref, sem.at[0])
    fetch_h = [
        pltpu.make_async_copy(h_hbm.at[BS * i : BS * (i + 1), :], h_ref.at[BS * i : BS * (i + 1), :], sem.at[1 + i])
        for i in range(6)
    ]
    fetch_pat.start()
    for copy in fetch_h:
        copy.start()
    fetch_pat.wait()
    pat = pat_ref[...].astype(F32)
    owner = lax.broadcasted_iota(jnp.int32, (12, 12 * BS), 1) // BS
    spread = (owner == lax.broadcasted_iota(jnp.int32, (12, 12 * BS), 0)).astype(F32)
    mask = stack(dot(pat, spread), jnp.zeros((2, 12 * BS), F32))
    mask_ref[...] = mask
    side = odd()
    for start, part in ((320, mask[:, 64:448]), (328, lanes(mask[:, 448:768], zeros(8, 1)))):
        b_ref[start : start + 8, :] = part
        a_ref[start : start + 8, :] = part
    total = jnp.zeros((8, 128), F32)
    rows = []
    for i in range(6):
        at = slice(BS * i, BS * (i + 1))
        fetch_h[i].wait()
        row = h_ref[at, :] * mask[i : i + 1, :]
        m_ref[at, :] = row
        square = row * row
        for a in range(8):
            for b in range(6):
                total = total + square[8 * a : 8 * a + 8, 128 * b : 128 * b + 128]
        rows.append(row)
    ssq_ref[...] = jnp.zeros(ssq_ref.shape, F32) + jnp.sum(total)
    for i in range(5):
        at = slice(BS * i, BS * (i + 1))
        to_right, to_left = rows[i + 1][:, 64:448], rows[i][:, 384:768]
        b_ref[at, :] = jnp.where(side, to_right, to_left)
        a_ref[at, :] = jnp.where(side, to_left, to_right)


def copy_all(sem, *pairs):
    copies = [pltpu.make_async_copy(source, target, sem.at[i]) for i, (source, target) in enumerate(pairs)]
    for copy in copies:
        copy.start()
    return copies


def halos(across_ref, inside_ref):
    side = odd()
    fb, fa = across_ref[...], inside_ref[...]
    return jnp.where(side, fa, fb), jnp.where(side, fb, fa)


def surroundings(own, fl, fr, g):
    fl, fr = fl[0:320] * g, fr[0:320] * g
    low = stack(*[lanes(zeros(BS, i), fl[BS * i : BS * (i + 1)], zeros(BS, 4 - i)) for i in range(5)])
    high = stack(*[lanes(zeros(BS, i), fr[BS * i : BS * (i + 1)], zeros(BS, 4 - i)) for i in range(5)])
    cross_l = own[:, 0:384].T[0:320]
    cross_r = own[:, 640:1024].T[64:384]
    hl = lanes(zeros(320, 1), low[:, 0:320], mirror(low[:, 320:640], True), cross_l[:, 0:320])
    hr = lanes(cross_r[:, 64:384], mirror(high[:, 0:320], False), high[:, 320:640], zeros(320, 1))
    return hl, hr


def masks(mask_own, fl, fr):
    mask_l, mask_r = [], []
    for i in range(5):
        band = lanes(fl[321 + i : 322 + i], fl[329 + i : 330 + i, 0:320])
        mask_l.append(lanes(zeros(1, 1 + i), band, zeros(1, 4 - i))[:, 384:1024])
        band = lanes(fr[320 + i : 321 + i], fr[328 + i : 329 + i, 0:320])
        mask_r.append(lanes(zeros(1, i), band, zeros(1, 5 - i))[:, 0:640])
    return own_window(mask_own), stack(*mask_l), stack(*mask_r)


def square_kernel(
    m_ref, mask_ref, b_ref, a_ref, ssq_ref,
    hl_hbm, hr_hbm, s_ref, ko_ref, kl_ref, kr_ref, top_ref, sb_ref, sa_ref, sum_ref,
    oh, ol, wh, wl, hl_ref, hr_ref, sem,
):
    sum_ref[...] = jnp.zeros(sum_ref.shape, F32) + jnp.sum(ssq_ref[...]) / 128.0
    fl, fr = halos(b_ref, a_ref)
    m = m_ref[...]
    top = jnp.maximum(jnp.max(jnp.abs(fl[0:320])), jnp.max(jnp.abs(fr[0:320])))
    top = jnp.maximum(jnp.maximum(top, jnp.max(jnp.abs(m))), 1e-11)
    top_ref[...] = jnp.zeros(top_ref.shape, F32) + top
    mask_o, mask_l, mask_r = masks(mask_ref[...], fl, fr)
    ko_ref[...] = stack(mask_o, jnp.zeros((2, 1024), F32))
    kl_ref[...] = stack(mask_l, jnp.zeros((3, 640), F32))
    kr_ref[...] = stack(mask_r, jnp.zeros((3, 640), F32))
    own = own_window(m) * (1.0 / top)
    hl, hr = surroundings(own, fl, fr, 1.0 / top)
    hl_ref[...] = hl
    hr_ref[...] = hr
    copies = copy_all(sem, (hl_ref, hl_hbm), (hr_ref, hr_hbm))
    store((oh, ol), 0, own)
    store((wh, wl), 0, lanes(hl[:, 384:1024], zeros(320, 6)))
    wh[320:704, :], wl[320:704, :] = oh[...], ol[...]
    store((wh, wl), 704, lanes(zeros(320, 6), hr[:, 0:640]))
    s = masked_rows(own_product((oh, ol), (wh, wl)), mask_o)
    s_ref[...] = narrow(s)
    side = odd()
    scale = zeros(BS, 3) + top
    row = [s[BS * i : BS * (i + 1)] for i in range(6)]
    to_right = stack(
        lanes(row[1][:, 64:384], row[5][:, 320:384]),
        lanes(row[2][:, 128:384], row[4][:, 256:384]),
        lanes(row[3][:, 192:384], scale),
    )
    to_left = stack(
        lanes(row[4][:, 640:960], row[0][:, 640:704]),
        lanes(row[3][:, 640:896], row[1][:, 640:768]),
        lanes(row[2][:, 640:832], scale),
    )
    sb_ref[...] = jnp.where(side, to_right, to_left)
    sa_ref[...] = jnp.where(side, to_left, to_right)
    for copy in copies:
        copy.wait()


def second_kernel(
    norms_ref, top_ref, s_ref, ko_ref, kl_ref, kr_ref, h_hbm, hl_hbm, hr_hbm,
    hl_h, hl_l, hr_h, hr_l, wh, wl, near_l, near_r, x_ref, xh, xl, s2_ref, b_ref, a_ref, scal_ref,
    oh, ol, hl_ref, hr_ref, h_ref, sem, *, size
):
    copies = copy_all(sem, (h_hbm, h_ref), (hl_hbm, hl_ref), (hr_hbm, hr_ref))
    s = widen(s_ref[...])
    store((wh, wl), 320, s)
    copies[0].wait()
    own = masked_rows(own_window(h_ref[...]), ko_ref[0:6, :] * (1.0 / top_ref[0:1, 0:1]))
    store((oh, ol), 0, own)
    copies[1].wait()
    hl = hl_ref[...]
    store((hl_h, hl_l), 0, hl)
    s_l = masked_rows(gram(hl_h[...], hl_l[...]), kl_ref[0:5, 0:320])
    copies[2].wait()
    hr = hr_ref[...]
    store((hr_h, hr_l), 0, hr)
    s_r = masked_rows(gram(hr_h[...], hr_l[...]), kr_ref[0:5, 320:640])

    store((wh, wl), 0, lanes(s_l, s[:, 0:384].T[0:320, 0:320], zeros(320, 6)))
    store((wh, wl), 704, lanes(zeros(320, 6), s[:, 640:1024].T[64:384, 64:384], s_r))
    t_o = masked_rows(own_product((oh, ol), (wh, wl)), ko_ref[0:6, :])
    near_l[...] = hl[:, 384:704]
    near_r[...] = hr[:, 320:640]
    t_l = cross_left((hl_h[:, 384:1024], hl_l[:, 384:1024]), (wh, wl))
    t_l = masked_rows(t_l, kl_ref[0:5, 320:640])
    t_r = cross_right((hr_h[:, 0:640], hr_l[:, 0:640]), (wh, wl))
    t_r = masked_rows(t_r, kr_ref[0:5, 0:320])

    frob = jnp.sqrt(jnp.sum(norms_ref[...], keepdims=True)[0] / 128.0)
    inverse = 3.0 * frob / size
    r = top_ref[0:1, 0:1] / inverse
    c1 = 1.5 * r
    c3 = 0.5 * r * r * r
    for i, value in enumerate((inverse, c1, c3)):
        scal_ref[8 * i : 8 * i + 8, :] = jnp.zeros((8, 128), F32) + value
    x = c1 * own - c3 * t_o
    x_ref[...] = x
    store((xh, xl), 0, lanes(zeros(320, 5), c1 * hl[:, 704:1024] - c3 * t_l, zeros(320, 6)))
    store((xh, xl), 320, x)
    store((xh, xl), 704, lanes(zeros(320, 6), c1 * hr[:, 0:320] - c3 * t_r, zeros(320, 5)))
    s2 = []
    for p in range(3):
        rows, reach = slice(320 + 128 * p, 448 + 128 * p), slice(128 * p, 128 * p + 768)
        s2.append(dot3(xh[rows, reach], xl[rows, reach], xh[reach, 256:768], xl[reach, 256:768]))
    s2 = masked_rows(stack(*s2), ko_ref[0:6, 256:768])[:, 64:448]
    s2_ref[...] = s2

    def pack(block):
        tail = lanes(block[0:160, 256:320], block[160:320, 256:320])
        return stack(block[:, 0:128], block[:, 128:256], tail)

    side = odd()
    to_right, to_left = pack(s2[64:384, 64:384]), pack(s2[0:320, 0:320])
    b_ref[...] = jnp.where(side, to_right, to_left)
    a_ref[...] = jnp.where(side, to_left, to_right)


def third_kernel(
    x_ref, xh, xl, s2_ref, hl_h, hl_l, hr_h, hr_l, sh, sl, near_l, near_r, fb_ref, fa_ref, top_ref, scal_ref,
    ko_ref, kl_ref, kr_ref, out_ref, wh, wl
):
    top = top_ref[0:1, 0:1]
    inverse, c1, c3 = scal_ref[0:1, 0:1], scal_ref[8:9, 0:1], scal_ref[16:17, 0:1]
    fl, fr = halos(fb_ref, fa_ref)
    far_l = stack(
        fl[0:64, 0:320],
        lanes(zeros(BS, 1), fl[64:128, 0:256]),
        lanes(zeros(BS, 2), fl[128:192, 0:192]),
        lanes(zeros(BS, 3), fl[64:128, 256:384]),
        lanes(zeros(BS, 4), fl[0:64, 320:384]),
    )
    far_r = stack(
        lanes(fr[0:64, 320:384], zeros(BS, 4)),
        lanes(fr[64:128, 256:384], zeros(BS, 3)),
        lanes(fr[128:192, 0:192], zeros(BS, 2)),
        lanes(fr[64:128, 0:256], zeros(BS, 1)),
        fr[0:64, 0:320],
    )
    ratio_l, ratio_r = fl[128:129, 192:193] / top, fr[128:129, 192:193] / top
    far_h, far_s = split(stack(zeros(64, 6), lanes((far_l * ratio_l * ratio_l).T, zeros(320, 1))))
    right_h, right_l = stack(far_h, sh[0:640, 0:384]), stack(far_s, sl[0:640, 0:384])
    t_l = dot3(hl_h[...], hl_l[...], right_h, right_l)[:, 0:320]
    far_h, far_s = split(stack(lanes(zeros(320, 1), (far_r * ratio_r * ratio_r).T), zeros(64, 6)))
    right_h, right_l = stack(sh[384:1024, 640:1024], far_h), stack(sl[384:1024, 640:1024], far_s)
    t_r = dot3(hr_h[...], hr_l[...], right_h, right_l)[:, 64:384]
    xl_h, xl_l = split(c1 * near_l[...] - c3 * masked_rows(t_l, kl_ref[0:5, 0:320]))
    xr_h, xr_l = split(c1 * near_r[...] - c3 * masked_rows(t_r, kr_ref[0:5, 320:640]))

    ah, al = xh[320:704, :], xl[320:704, :]
    right_h = stack(lanes(xl_h, xh[0:320, 320:384]), xh[320:704, 0:384])
    right_l = stack(lanes(xl_l, xl[0:320, 320:384]), xl[320:704, 0:384])
    s2_a = []
    for p in range(3):
        rows, reach = slice(128 * p, 128 * p + 128), slice(128 * p, 640)
        part = dot3(ah[rows, reach], al[rows, reach], right_h[reach, 128 * p :], right_l[reach, 128 * p :])
        s2_a.append(lanes(zeros(128, 2 * p), part))
    s2_a = masked_rows(stack(*s2_a), ko_ref[0:6, 0:384])
    right_h = stack(xh[320:704, 640:1024], lanes(xh[704:1024, 640:704], xr_h))
    right_l = stack(xl[320:704, 640:1024], lanes(xl[704:1024, 640:704], xr_l))
    s2_b = []
    for p in range(3):
        rows, reach, end = slice(128 * p, 128 * p + 128), slice(384, 768 + 128 * p), 128 * (p + 1)
        inner = slice(64, 448 + 128 * p)
        part = dot3(ah[rows, reach], al[rows, reach], right_h[inner, 0:end], right_l[inner, 0:end])
        s2_b.append(lanes(part, zeros(128, 4 - 2 * p)))
    s2_b = masked_rows(stack(*s2_b), ko_ref[0:6, 640:1024])
    left_h, left_l = lanes(xl_h, xh[0:320, 320:640]), lanes(xl_l, xl[0:320, 320:640])
    s2_l = masked_rows(cross_left((left_h, left_l), (xh, xl)), kl_ref[0:5, 320:640])
    left_h, left_l = lanes(xh[704:1024, 384:704], xr_h), lanes(xl[704:1024, 384:704], xr_l)
    s2_r = masked_rows(cross_right((left_h, left_l), (xh, xl)), kr_ref[0:5, 0:320])
    store((wh, wl), 0, lanes(zeros(320, 5), s2_l, zeros(320, 6)))
    store((wh, wl), 320, lanes(s2_a[:, 0:320], s2_ref[...], s2_b[:, 64:384]))
    store((wh, wl), 704, lanes(zeros(320, 6), s2_r, zeros(320, 5)))
    cubic = own_product((xh.at[320:704, :], xl.at[320:704, :]), (wh, wl))
    for i in range(6):
        at = slice(BS * i, BS * (i + 1))
        row = (1.5 * x_ref[at, :] - 0.5 * (cubic[at] * ko_ref[i : i + 1, :])) * inverse
        if i == 0:
            out_ref[at, :] = lanes(zeros(BS, 1), row[:, 0:704])
        else:
            out_ref[at, :] = row[:, 64 * (i - 1) : 64 * (i - 1) + 768]


def last_kernel(part_ref, xh, xl, ko_ref, scal_ref, fb_ref, fa_ref, out_hbm, out_ref, sem):
    corner_l, corner_r = [
        lanes(f[0:320], f[320:640], stack(f[640:800, 0:64], f[640:800, 64:128]))
        for f in halos(fb_ref, fa_ref)
    ]
    half = 0.5 * scal_ref[0:1, 0:1]
    corner_l = stack(lanes(corner_l, zeros(320, 1)), zeros(64, 6))
    corner_r = stack(zeros(64, 6), lanes(zeros(320, 1), corner_r))
    ch, cl = split(corner_l)
    near = dot3(xh[448:640, 128:384], xl[448:640, 128:384], ch[128:384, 128:384], cl[128:384, 128:384])
    add_l = stack(dot3(xh[320:448, 0:384], xl[320:448, 0:384], ch, cl), lanes(zeros(192, 2), near))
    ch, cl = split(corner_r)
    near = dot3(xh[384:576, 640:896], xl[384:576, 640:896], ch[0:256, 0:256], cl[0:256, 0:256])
    add_r = stack(lanes(near, zeros(192, 2)), dot3(xh[576:704, 640:1024], xl[576:704, 640:1024], ch, cl))
    copies = []
    for i in range(6):
        at = slice(BS * i, BS * (i + 1))
        parts = []
        if i < 5:
            part = add_l[at, 64 * i : 320] * (half * ko_ref[i : i + 1, 64 * i : 320])
            parts.append(lanes(zeros(BS, 1), part))
        parts.append(zeros(BS, 12 - (6 - i if i < 5 else 0) - i))
        if i > 0:
            part = add_r[BS * (i - 1) : BS * i, 64 : 64 + 64 * i]
            parts.append(part * (half * ko_ref[i : i + 1, 704 : 704 + 64 * i]))
        out_ref[at, :] = part_ref[at, :] - lanes(*parts)
        copies.append(pltpu.make_async_copy(out_ref.at[at, :], out_hbm.at[at, :], sem.at[i]))
        copies[-1].start()
    for copy in copies:
        copy.wait()


def call(kernel, outs, args, flops, name, mib, scratch=(), in_hbm=(), out_hbm=()):
    args = [pltpu.with_memory_space_constraint(a, pltpu.HBM) if i in in_hbm else a for i, a in enumerate(args)]
    return pl.pallas_call(
        kernel,
        out_shape=[(pltpu.HBM if i in out_hbm else pltpu.VMEM)(s, t) for i, (s, t) in enumerate(outs)],
        in_specs=[HBM if i in in_hbm else VMEM for i in range(len(args))],
        out_specs=[HBM if i in out_hbm else VMEM for i in range(len(outs))],
        scratch_shapes=list(scratch),
        compiler_params=pltpu.CompilerParams(vmem_limit_bytes=mib << 20),
        cost_estimate=pl.CostEstimate(flops=flops, bytes_accessed=1 << 20, transcendentals=0),
        name=name,
    )(*args)


def local(hamiltonian, pattern):
    n_blk, n_rep = lax.axis_size("blk"), lax.axis_size("rep")
    size = math.sqrt(n_blk * n_rep * 6 * BS)
    band = hamiltonian.reshape(6 * BS, 12 * BS)
    own, halo, corner, full = ((384, 1024), F32), ((320, 1024), F32), ((320, 320), F32), ((1024, 1024), BF16)
    mask_o, mask_h, scalar = ((8, 1024), F32), ((8, 640), F32), ((8, 128), F32)
    rows, far = ((384, 1024), BF16), ((192, 384), F32)
    dma = pltpu.SemaphoreType.DMA((2,))

    m, mask, to_b, to_a, ssq = call(
        prepare_kernel,
        [((384, 768), F32), ((8, 768), F32), ((336, 384), F32), ((336, 384), F32), ((n_rep, 1, 128), F32)],
        (band, pattern), 10**7, "prepare", 16,
        scratch=[pltpu.VMEM((384, 768), F32), pltpu.VMEM((6, 12), jnp.int32), pltpu.SemaphoreType.DMA((7,))],
        in_hbm=(0, 1),
    )
    first_b, first_a = across(to_b), inside(to_a)
    ssq = lax.all_to_all(ssq, "rep", 0, 0)
    wide = pltpu.VMEM((1024, 1024), BF16)
    hl, hr, s, ko, kl, kr, top, to_b, to_a, ssq = call(
        square_kernel,
        [halo, halo, ((384, 768), F32), mask_o, mask_h, mask_h, scalar, far, far, ((n_blk, 1, 128), F32)],
        (m, mask, first_b, first_a, ssq), 10**9, "first_square", 20,
        scratch=[pltpu.VMEM(*rows)] * 2 + [wide] * 2 + [pltpu.VMEM(*halo), pltpu.VMEM(*halo), dma], out_hbm=(0, 1),
    )
    far_b, far_a = across(to_b), inside(to_a)
    ssq = lax.all_to_all(ssq, "blk", 0, 0)
    pair = ((320, 1024), BF16)
    *operands, x, xh, xl, s2, to_b, to_a, scalars = call(
        lambda *refs: second_kernel(*refs, size=size),
        [pair, pair, pair, pair, full, full, corner, corner, own, full, full, ((384, 384), F32),
         ((800, 128), F32), ((800, 128), F32), ((24, 128), F32)],
        (ssq, top, s, ko, kl, kr, band, hl, hr), 10**10, "second_square", 24,
        scratch=[pltpu.VMEM(*rows)] * 2 + [pltpu.VMEM(*halo)] * 2
        + [pltpu.VMEM((384, 768), F32), pltpu.SemaphoreType.DMA((3,))],
        in_hbm=(6, 7, 8),
    )
    from_b, from_a = across(to_b), inside(to_a)
    (part,) = call(
        third_kernel, [((384, 768), F32)],
        (x, xh, xl, s2, *operands, far_b, far_a, top, scalars, ko, kl, kr),
        5 * 10**9, "second_cubic", 24, scratch=[wide, wide],
    )
    (out,) = call(
        last_kernel, [((384, 768), F32)], (part, xh, xl, ko, scalars, from_b, from_a), 10**9, "result", 16,
        scratch=[pltpu.VMEM((384, 768), F32), pltpu.SemaphoreType.DMA((6,))], out_hbm=(0,),
    )
    return out.reshape(6, BS, 12 * BS)


def solution(mesh):
    placed = (P(AXES, None, None), P(AXES, None))
    return jax.shard_map(
        local, mesh=mesh, in_specs=placed, out_specs=P(AXES, None, None), check_vma=False
    )
```
